32 devices in a mesh: groups: 2 (over y), space: 4 (over z), sample: 4 (over x, core).
Axes of the slice: x: 2, y: 2, z: 4, core: 2. Of those that a mesh axis runs over, the one named last changes fastest.
Arguments:
- tokens: bfloat16 [8, 4, 512, 512], P(('groups', 'sample'), 'space'), parts along dimension 0, may hold values from -6 to 6
- cotangent: bfloat16 [8, 4, 512, 512], P(('groups', 'sample'), 'space'), parts along dimension 0, may hold values from -6 to 6
- weight: bfloat16 [1024, 1536], P('groups'), parts along dimension 0
- margins: int32 [8, 4], P(('groups', 'sample')), parts along dimension 0, may hold values from 0 to 12, as said below
Outputs:
- attention: bfloat16 [8, 4, 512, 512], P(('groups', 'sample'), 'space'), parts along dimension 0
- token_grad: bfloat16 [8, 4, 512, 512], P(('groups', 'sample'), 'space'), parts along dimension 0
- weight_grad: float32 [1024, 1536], P(('groups', 'space'), 'sample'), parts along dimension 0
The draws below stay inside these ranges and needn't reach their ends.
There are 2 independent parts, one for each index of `groups`. The reference program is written for one: setup_inputs(seed, part) draws one part's arguments, and reference() takes and returns one part's arrays. A program takes and returns all parts, laid end to end along the dimension named above; each array names one. Nothing has to cross between parts.
Inputs may be any that keep to these rules, and one draw needn't show every extreme that they name: `margins`: some entry equals 12 and some entry is 0.
All inputs are finite; a program needn't handle non-finite values.
Results may differ from the reference program's by a relative error of at most 0.005.
Values may be sent and summed in bfloat16 or wider, within the bound.
No kernel may reach another device: no remote copies, remote signals or barrier semaphores. Data moves between devices by JAX's collectives and lax.ppermute only.
A program may use at most 64 MiB of HBM per device.

```python
import math
import jax
import jax.numpy as jnp
from jax import lax

D = 512
HEADS = 8
TH = 16
TW = 32
HALO = 3
MARGIN = 12
EVENTS = 4
TILES = 4
GRID_W = 4
GRID_H = 1
PH = 16
PW = 128


def draw_weight(key, part):
    key_base = jax.random.fold_in(key, 0)
    drawn = jax.random.normal(key_base, (D, 3 * D), jnp.float32) * D ** (-0.5)
    return drawn.astype(jnp.bfloat16)


def draw_margins(key, part):
    key_vals, key_high, key_low = jax.random.split(jax.random.fold_in(key, 7), 3)
    drawn = jax.random.randint(key_vals, (EVENTS * 4,), 0, MARGIN + 1, jnp.int32)
    high_slot = jax.random.randint(key_high, (), 0, EVENTS * 4, jnp.int32)
    low_slot = (high_slot + 1 + jax.random.randint(key_low, (), 0, EVENTS * 4 - 1, jnp.int32)) % (EVENTS * 4)
    drawn = drawn.at[high_slot].set(MARGIN).at[low_slot].set(0)
    return drawn.reshape(EVENTS, 4)


def shard_levels(key, dims, shards, least, largest):
    level = 1.0
    for axis_at, blocks in shards:
        heights = jax.random.uniform(jax.random.fold_in(jax.random.fold_in(key, 6), axis_at), (blocks,), jnp.float32, least / len(shards), largest / len(shards))
        level = level * jnp.repeat(jnp.exp(heights), dims[axis_at] // blocks).reshape((-1,) + (1,) * (len(dims) - 1 - axis_at))
    return level


def bell_draw(rng, extent, width, limit, pieces=(), held_as=jnp.bfloat16):
    values = width * jax.random.normal(rng, extent, jnp.float32)
    if pieces:
        values = values * shard_levels(rng, extent, pieces, -0.22, 0.18)
    return jnp.clip(values, -limit, limit).astype(held_as)


def setup_inputs(seed: int = 0, part: int = 0) -> dict:
    splits = jax.random.split(jax.random.key(seed), 5)
    part_keys = jax.random.split(jax.random.fold_in(splits[4], part), 5)
    tokens = bell_draw(part_keys[0], (EVENTS, TILES, TH * TW, D), 1.0, 6.0, ((0, 4), (1, 4)))
    cotangent = bell_draw(part_keys[1], (EVENTS, TILES, TH * TW, D), 1.0, 6.0, ((0, 4), (1, 4)))
    weight = draw_weight(jax.random.fold_in(jax.random.fold_in(splits[4], part), 71), part)
    margins = draw_margins(jax.random.fold_in(jax.random.fold_in(splits[4], part), 71), part)
    return dict(tokens=tokens, cotangent=cotangent, weight=weight, margins=margins)


def key_mask(tile_row, tile_col, margin_set, plane_rows, plane_cols):
    win_rows = TH + 2 * HALO
    win_cols = TW + 2 * HALO
    flat_keys = jnp.arange(win_rows * win_cols, dtype=jnp.int32)
    key_row = flat_keys // win_cols - HALO
    key_col = flat_keys % win_cols - HALO
    global_row = tile_row * TH + key_row
    global_col = tile_col * TW + key_col
    inside = (global_row >= 0) & (global_row < plane_rows) & (global_col >= 0) & (global_col < plane_cols)
    living = (global_row >= margin_set[0]) & (global_row < plane_rows - margin_set[1]) & (global_col >= margin_set[2]) & (global_col < plane_cols - margin_set[3])
    flat_query = jnp.arange(TH * TW, dtype=jnp.int32)
    itself = (key_row[None, :] == (flat_query // TW)[:, None]) & (key_col[None, :] == (flat_query % TW)[:, None])
    return inside[None, :] & (living[None, :] | itself)

def head_pass(query, window_kv, cotangent, allowed, head_index, head_size, feat_width):
    offset = head_index * head_size
    contract_last = (((1,), (1,)), ((), ()))
    contract_first = (((0,), (0,)), ((), ()))
    query_head = lax.dynamic_slice_in_dim(query, offset, head_size, 1)
    key_head = lax.dynamic_slice_in_dim(window_kv, offset, head_size, 1)
    value_head = lax.dynamic_slice_in_dim(window_kv, feat_width + offset, head_size, 1)
    cotan_head = lax.dynamic_slice_in_dim(cotangent, offset, head_size, 1)
    scaling = 1.0 / math.sqrt(head_size)
    scores = lax.dot_general(query_head, key_head, contract_last, preferred_element_type=jnp.float32) * scaling
    scores = jnp.where(allowed, scores, -1e+30)
    highest = lax.optimization_barrier(jnp.max(scores, axis=1, keepdims=True))
    unnormed = jnp.exp(scores - highest)
    prob_full = unnormed / lax.optimization_barrier(jnp.sum(unnormed, axis=1, keepdims=True))
    prob_half = prob_full.astype(jnp.bfloat16)
    head_attend = jnp.dot(prob_half, value_head, preferred_element_type=jnp.float32).astype(jnp.bfloat16)
    grad_prob = lax.dot_general(cotan_head, value_head, contract_last, preferred_element_type=jnp.float32)
    row_delta = lax.optimization_barrier(jnp.sum(prob_full * grad_prob, axis=1, keepdims=True))
    grad_score = (prob_full * (grad_prob - row_delta) * scaling).astype(jnp.bfloat16)
    query_delta = jnp.dot(grad_score, key_head, preferred_element_type=jnp.float32)
    key_delta = lax.dot_general(grad_score, query_head, contract_first, preferred_element_type=jnp.float32)
    value_delta = lax.dot_general(prob_half, cotan_head, contract_first, preferred_element_type=jnp.float32)
    return (head_attend, query_delta, key_delta, value_delta)

def tile_pass(query, window_kv, cotangent, allowed):
    feat_width = query.shape[1]
    head_size = feat_width // HEADS

    def one_head(head_index, carry):
        attended, grad_query, grad_window = carry
        head_attend, query_delta, key_delta, value_delta = head_pass(query, window_kv, cotangent, allowed, head_index, head_size, feat_width)
        offset = head_index * head_size
        attended = lax.dynamic_update_slice_in_dim(attended, head_attend, offset, 1)
        grad_query = lax.dynamic_update_slice_in_dim(grad_query, query_delta, offset, 1)
        grad_window = lax.dynamic_update_slice_in_dim(grad_window, key_delta, offset, 1)
        grad_window = lax.dynamic_update_slice_in_dim(grad_window, value_delta, feat_width + offset, 1)
        return (attended, grad_query, grad_window)
    start_carry = (jnp.zeros(query.shape, jnp.bfloat16), jnp.zeros(query.shape, jnp.float32), jnp.zeros(window_kv.shape, jnp.float32))
    return lax.fori_loop(0, HEADS, one_head, start_carry)

def reference(tokens, cotangent, weight, margins):
    feat_width = weight.shape[0]
    win_rows = TH + 2 * HALO
    win_cols = TW + 2 * HALO
    tok_float = tokens.astype(jnp.float32)
    centred = tok_float - lax.optimization_barrier(jnp.mean(tok_float, axis=-1, keepdims=True))
    inv_scale = lax.rsqrt(lax.optimization_barrier(jnp.mean(centred * centred, axis=-1, keepdims=True)) + 1e-05)
    standard = centred * inv_scale
    normed = standard.astype(jnp.bfloat16)
    flat_normed = normed.reshape(-1, feat_width)
    projected = jnp.dot(flat_normed, weight, preferred_element_type=jnp.float32).astype(jnp.bfloat16)
    projected = projected.reshape(EVENTS, TILES, TH * TW, 3 * feat_width)
    queries = projected[..., :feat_width]
    key_value = projected[..., feat_width:]
    key_plane = key_value.reshape(EVENTS, GRID_H, GRID_W, TH, TW, 2 * feat_width).transpose(0, 1, 3, 2, 4, 5).reshape(EVENTS, PH, PW, 2 * feat_width)
    padded = jnp.pad(key_plane, ((0, 0), (HALO, HALO), (HALO, HALO), (0, 0)))
    zero_index = jnp.zeros((), jnp.int32)
    attended_all = []
    grad_qkv_all = []
    for event_number in range(EVENTS):
        padded_event = padded[event_number]
        margin_set = margins[event_number]

        def tile_step(accumulated, inputs):
            tile_index, query_tile, cotan_tile = inputs
            tile_row = tile_index // GRID_W
            tile_col = tile_index % GRID_W
            corner = (tile_row * TH, tile_col * TW, zero_index)
            window = lax.dynamic_slice(padded_event, corner, (win_rows, win_cols, 2 * feat_width))
            allowed = key_mask(tile_row, tile_col, margin_set, PH, PW)
            attended, grad_query, grad_window = tile_pass(query_tile, window.reshape(-1, 2 * feat_width), cotan_tile, allowed)
            current = lax.dynamic_slice(accumulated, corner, (win_rows, win_cols, 2 * feat_width))
            accumulated = lax.dynamic_update_slice(accumulated, current + grad_window.reshape(win_rows, win_cols, 2 * feat_width), corner)
            return (accumulated, (attended, grad_query))
        accumulated = jnp.zeros((PH + 2 * HALO, PW + 2 * HALO, 2 * feat_width), jnp.float32)
        accumulated, (attended, grad_query) = lax.scan(tile_step, accumulated, (jnp.arange(TILES, dtype=jnp.int32), queries[event_number], cotangent[event_number]))
        own_grad = accumulated[HALO:HALO + PH, HALO:HALO + PW].reshape(GRID_H, TH, GRID_W, TW, 2 * feat_width).transpose(0, 2, 1, 3, 4).reshape(TILES, TH * TW, 2 * feat_width)
        attended_all.append(attended)
        grad_qkv_all.append(jnp.concatenate([grad_query, own_grad], axis=-1).astype(jnp.bfloat16))
    attention = jnp.stack(attended_all)
    grad_qkv = jnp.stack(grad_qkv_all).reshape(-1, 3 * feat_width)
    weight_grad = lax.dot_general(flat_normed, grad_qkv, (((0,), (0,)), ((), ())), preferred_element_type=jnp.float32)
    grad_normed = lax.dot_general(grad_qkv, weight, (((1,), (1,)), ((), ())), preferred_element_type=jnp.float32).reshape(tokens.shape)
    grad_mean = lax.optimization_barrier(jnp.mean(grad_normed, axis=-1, keepdims=True))
    grad_cross = lax.optimization_barrier(jnp.mean(grad_normed * standard, axis=-1, keepdims=True))
    token_grad = ((grad_normed - grad_mean - standard * grad_cross) * inv_scale).astype(jnp.bfloat16)
    return (attention, token_grad, weight_grad)
```

```python
import functools
import math

import jax
import jax.numpy as jnp
import numpy as np
from jax import lax
from jax.experimental import pallas as pl
from jax.experimental.pallas import tpu as pltpu
from jax.sharding import PartitionSpec as P

HEADS = 8
HEAD = 64
TH = 16
TW = 32
HALO = 3
TOKENS = TH * TW
NEG = -1e30
LAST = (((1,), (1,)), ((), ()))
F32 = jnp.float32
BF16 = jnp.bfloat16
GROUPS = ((0, 1, 2, 3), (4, 5, 6, 7))
CHUNK = 256

vmem = functools.partial(pl.BlockSpec, memory_space=pltpu.VMEM)
smem = functools.partial(pl.BlockSpec, memory_space=pltpu.SMEM)


def params():
    return pltpu.CompilerParams(vmem_limit_bytes=40 * 1024 * 1024)


def dot(a, b):
    return jnp.dot(a, b, preferred_element_type=F32)


def dot_t(a, b):
    return lax.dot_general(a, b, LAST, preferred_element_type=F32)


def normalise(tok):
    tok = tok.astype(F32)
    centred = tok - jnp.mean(tok, axis=-1, keepdims=True)
    inv = lax.rsqrt(jnp.mean(centred * centred, axis=-1, keepdims=True) + 1e-05)
    return centred * inv, inv


def permutation(feat, bits, scal_ref):
    blocks = 1 << bits
    size = feat // blocks
    row = lax.broadcasted_iota(jnp.int32, (feat, feat), 0)
    col = lax.broadcasted_iota(jnp.int32, (feat, feat), 1)
    relative = row // size
    actual = jnp.zeros_like(row)
    for i in range(bits):
        actual = actual | (((relative >> (bits - 1 - i)) & 1) << i)
    actual = actual ^ scal_ref[0]
    source = actual * size + row % size
    return jnp.where(col == source, 1.0, 0.0).astype(BF16)


def kernel_own(bits, scal_ref, tok_ref, w_ref, q_ref, kv_ref, kvt_ref, nt_ref, bias_ref):
    feat = w_ref.shape[0]
    standard, _ = normalise(tok_ref[...])
    normed = standard.astype(BF16)
    scale = 1.0 / math.sqrt(HEAD)
    q_ref[...] = (dot(normed, w_ref[:, :feat]).astype(BF16).astype(F32) * scale).astype(BF16)
    for i in range(2):
        part = dot(normed, w_ref[:, (i + 1) * feat : (i + 2) * feat]).astype(BF16)
        kv_ref[:, i * feat : (i + 1) * feat] = part
        kvt_ref[i * feat : (i + 1) * feat, :] = part.T
    nt_ref[...] = dot_t(permutation(feat, bits, scal_ref), normed).astype(BF16)
    key = lax.broadcasted_iota(jnp.int32, (TOKENS, TOKENS), 0)
    query = lax.broadcasted_iota(jnp.int32, (TOKENS, TOKENS), 1)
    row = scal_ref[1] + key // TW
    col = scal_ref[2] + key % TW
    live = (row >= scal_ref[3]) & (row < scal_ref[4]) & (col >= scal_ref[5]) & (col < scal_ref[6])
    bias_ref[...] = jnp.where(live | (key == query), 0.0, NEG)


def kernel_halo(bits, count, scal_ref, *refs):
    toks, (w_ref, kv_ref, kvt_ref, nt_ref) = refs[:count], refs[count:]
    feat = w_ref.shape[0]
    padded = kv_ref.shape[0]
    parts = [r[...].astype(F32) for r in toks]
    have = sum(p.shape[0] for p in parts)
    if have < padded:
        parts.append(jnp.zeros((padded - have, feat), F32))
    standard, _ = normalise(jnp.concatenate(parts, axis=0))
    normed = standard.astype(BF16)
    for i in range(2):
        part = dot(normed, w_ref[:, (i + 1) * feat : (i + 2) * feat]).astype(BF16)
        kv_ref[:, i * feat : (i + 1) * feat] = part
        kvt_ref[i * feat : (i + 1) * feat, :] = part.T
    nt_ref[...] = dot_t(permutation(feat, bits, scal_ref), normed).astype(BF16)


def kernel_attend(
    heads, first, spans, *refs
):
    refs = list(refs)
    (q_ref, kv_ref, kvt_ref, nt_ref, bias_ref, kvh_ref, kvht_ref, nht_ref, hbias_ref, cot_ref, w_ref) = refs[:11]
    refs = refs[11:]
    prior_ref = None if first else refs.pop(0)
    (att_ref, gq_ref, gk_ref, gv_ref, keep_ref, send_ref) = refs[:6]
    gnh_refs = refs[6 : 6 + len(spans)]
    (pb_s, ds_s, cm_s, qm_s, att_s, dqt_s, kvg_s) = refs[6 + len(spans) :]
    feat = w_ref.shape[0]
    width = len(heads) * HEAD
    lane = lax.broadcasted_iota(jnp.int32, (TOKENS, 2 * HEAD), 1)
    scale = 1.0 / math.sqrt(HEAD)
    for pair in range(len(heads) // 2):
        base = heads[2 * pair] * HEAD
        cols = slice(base, base + 2 * HEAD)
        vcols = slice(feat + base, feat + base + 2 * HEAD)
        q = q_ref[:, cols]
        cot = cot_ref[:, cols]
        k_own, k_halo = kv_ref[:, cols], kvh_ref[:, cols]
        v_own, v_halo = kv_ref[:, vcols], kvh_ref[:, vcols]
        zero = jnp.zeros_like(q)
        for odd in range(2):
            mine = (lane >= HEAD) if odd else (lane < HEAD)
            qm = jnp.where(mine, q, zero)
            cm = jnp.where(mine, cot, zero)
            qm_s[odd * TOKENS : (odd + 1) * TOKENS, :] = qm
            cm_s[odd * TOKENS : (odd + 1) * TOKENS, :] = cm
            krow = base + odd * HEAD
            vrow = feat + krow
            orow = (2 * pair + odd) * HEAD
            for c in range(TOKENS // CHUNK):
                lanes = slice(c * CHUNK, (c + 1) * CHUNK)
                out = slice(odd * TOKENS + c * CHUNK, odd * TOKENS + (c + 1) * CHUNK)
                qc, cc = qm[lanes, :], cm[lanes, :]
                s_own = dot_t(k_own, qc) + bias_ref[:, lanes]
                s_halo = dot_t(k_halo, qc) + hbias_ref[:, lanes]
                top = jnp.maximum(jnp.max(s_own, axis=0, keepdims=True), jnp.max(s_halo, axis=0, keepdims=True))
                e_own = jnp.exp(s_own - top)
                e_halo = jnp.exp(s_halo - top)
                inv = 1.0 / (jnp.sum(e_own, axis=0, keepdims=True) + jnp.sum(e_halo, axis=0, keepdims=True))
                p_own = e_own * inv
                p_halo = e_halo * inv
                pb_own = p_own.astype(BF16)
                pb_halo = p_halo.astype(BF16)
                pb_s[:TOKENS, out] = pb_own
                pb_s[TOKENS:, out] = pb_halo
                att_s[orow : orow + HEAD, lanes] = dot(kvt_ref[vrow : vrow + HEAD, :], pb_own) + dot(
                    kvht_ref[vrow : vrow + HEAD, :], pb_halo
                )
                g_own = dot_t(v_own, cc)
                g_halo = dot_t(v_halo, cc)
                delta = jnp.sum(p_own * g_own, axis=0, keepdims=True) + jnp.sum(
                    p_halo * g_halo, axis=0, keepdims=True
                )
                ds_own = (p_own * (g_own - delta)).astype(BF16)
                ds_halo = (p_halo * (g_halo - delta)).astype(BF16)
                ds_s[:TOKENS, out] = ds_own
                ds_s[TOKENS:, out] = ds_halo
                dqt_s[orow : orow + HEAD, lanes] = scale * (
                    dot(kvt_ref[krow : krow + HEAD, :], ds_own)
                    + dot(kvht_ref[krow : krow + HEAD, :], ds_halo)
                )
        pcols = slice(pair * 2 * HEAD, (pair + 1) * 2 * HEAD)
        kvg_s[:, pcols] = dot(ds_s[...], qm_s[...]).astype(BF16)
        kvg_s[:, width + pair * 2 * HEAD : width + (pair + 1) * 2 * HEAD] = dot(pb_s[...], cm_s[...]).astype(BF16)
    att_ref[...] = att_s[...].T.astype(BF16)
    dqt = dqt_s[...].astype(BF16)
    gq_ref[...] = dqt_s[...].T.astype(BF16)
    gk_ref[...] = kvg_s[:TOKENS, :width]
    gv_ref[...] = kvg_s[:TOKENS, width:]
    half = feat // 2
    for rows, target in ((slice(0, half), keep_ref), (slice(half, feat), send_ref)):
        nt = nt_ref[rows, :]
        target[:, :width] = dot_t(nt, dqt).astype(target.dtype)
        target[:, width:] = (dot(nt, kvg_s[:TOKENS, :]) + dot(nht_ref[rows, :], kvg_s[TOKENS:, :])).astype(
            target.dtype
        )
    base = heads[0] * HEAD
    gnh = dot_t(kvg_s[TOKENS:, :width], w_ref[:, feat + base : feat + base + width]) + dot_t(
        kvg_s[TOKENS:, width:], w_ref[:, 2 * feat + base : 2 * feat + base + width]
    )
    if prior_ref is not None:
        gnh = gnh + prior_ref[...]
    for (lo, hi), ref in zip(spans, gnh_refs):
        ref[...] = gnh[lo:hi, :].astype(ref.dtype)


def kernel_final(groups, count, tok_ref, w_ref, index_ref, *refs):
    grads = refs[: 3 * groups]
    arrived = refs[3 * groups : 3 * groups + count]
    out_ref = refs[3 * groups + count]
    feat = w_ref.shape[0]
    total = None
    for g in range(groups):
        width = grads[3 * g].shape[1]
        base = sum(grads[3 * i].shape[1] for i in range(g))
        for j in range(3):
            at = j * feat + base
            term = dot_t(grads[3 * g + j][...], w_ref[:, at : at + width])
            total = term if total is None else total + term
    padded = index_ref.shape[1]
    parts = [r[...].astype(F32) for r in arrived]
    have = sum(p.shape[0] for p in parts)
    if have < padded:
        parts.append(jnp.zeros((padded - have, feat), F32))
    rim = jnp.concatenate(parts, axis=0).astype(BF16)
    token = lax.broadcasted_iota(jnp.int32, (TOKENS, padded), 0)
    place = jnp.where(token == index_ref[...], 1.0, 0.0).astype(BF16)
    total = total + dot(place, rim)
    standard, inv = normalise(tok_ref[...])
    mean = jnp.mean(total, axis=-1, keepdims=True)
    cross = jnp.mean(total * standard, axis=-1, keepdims=True)
    out_ref[...] = ((total - mean - standard * cross) * inv).astype(BF16)


def shift(value, axis, steps):
    count = lax.axis_size(axis)
    first, last = max(0, -steps), min(count, count - steps)
    return lax.ppermute(value, axis, [(i, i + steps) for i in range(first, last)])


def swap(value, axis, bit):
    count = lax.axis_size(axis)
    return lax.ppermute(value, axis, [(i, i ^ (1 << bit)) for i in range(count)])


def span(step, length):
    if step < 0:
        return (length - HALO, length)
    if step > 0:
        return (0, HALO)
    return (0, length)


def window_span(step, length):
    if step < 0:
        return (-HALO, 0)
    if step > 0:
        return (length, length + HALO)
    return (0, length)


def struct(shape, dtype):
    return jax.ShapeDtypeStruct(shape, dtype)


def cost(flops, nbytes, exps=0):
    return pl.CostEstimate(flops=int(flops), bytes_accessed=int(nbytes), transcendentals=int(exps))


def local(tokens, cotangent, weight, margins):
    feat = weight.shape[0]
    tok, cot = tokens[0, 0], cotangent[0, 0]
    n_space, n_sample = lax.axis_size("space"), lax.axis_size("sample")
    grid_cols = min(8, n_space)
    grid_rows = n_space // grid_cols
    plane_rows, plane_cols = grid_rows * TH, grid_cols * TW
    position = lax.axis_index("space")
    member = lax.axis_index("sample")
    tile_row, tile_col = position // grid_cols, position % grid_cols
    row_steps = (-1, 0, 1) if grid_rows > 1 else (0,)
    steps = [(r, c) for r in row_steps for c in (-1, 0, 1) if (r, c) != (0, 0)]
    counts, key_rows, key_cols, sources = [], [], [], []
    for r, c in steps:
        wr, wc = window_span(r, TH), window_span(c, TW)
        sr, sc = span(r, TH), span(c, TW)
        rr, cc = np.meshgrid(np.arange(*wr), np.arange(*wc), indexing="ij")
        key_rows.append(rr.ravel())
        key_cols.append(cc.ravel())
        rr, cc = np.meshgrid(np.arange(*sr), np.arange(*sc), indexing="ij")
        sources.append((rr * TW + cc).ravel())
        counts.append(rr.size)
    halo = sum(counts)
    padded = -(-halo // 128) * 128
    fill = np.zeros(padded - halo, np.int64)
    key_rows = np.concatenate([*key_rows, fill]).astype(np.int32)[:, None]
    key_cols = np.concatenate([*key_cols, fill]).astype(np.int32)[:, None]
    rim_index = np.concatenate([*sources, fill - 1]).astype(np.int32)[None, :]
    valid = (np.arange(padded) < halo)[:, None]

    grid = tok.reshape(TH, TW, feat)
    halo_tokens = []
    for (r, c), n in zip(steps, counts):
        (r0, r1), (c0, c1) = span(r, TH), span(c, TW)
        piece = grid[r0:r1, c0:c1].reshape(n, feat)
        halo_tokens.append(shift(piece, "space", -(r * grid_cols + c)))

    margin = margins[0]
    bits = 1 + (n_space - 1).bit_length()
    me = position * 2 + (member & 1)
    scal = jnp.stack(
        [
            me,
            tile_row * TH,
            tile_col * TW,
            margin[0],
            plane_rows - margin[1],
            margin[2],
            plane_cols - margin[3],
        ]
    ).astype(jnp.int32)
    row, col = tile_row * TH + key_rows, tile_col * TW + key_cols
    open_key = (
        valid & (row >= 0) & (row < plane_rows) & (col >= 0) & (col < plane_cols)
        & (row >= margin[0]) & (row < plane_rows - margin[1])
        & (col >= margin[2]) & (col < plane_cols - margin[3])
    )
    hbias = jnp.broadcast_to(jnp.where(open_key, 0.0, NEG).astype(F32), (padded, TOKENS))

    q, kv, kvt, nt, bias = pl.pallas_call(
        functools.partial(kernel_own, bits),
        out_shape=(
            struct((TOKENS, feat), BF16),
            struct((TOKENS, 2 * feat), BF16),
            struct((2 * feat, TOKENS), BF16),
            struct((feat, TOKENS), BF16),
            struct((TOKENS, TOKENS), F32),
        ),
        in_specs=[smem(), vmem(), vmem()],
        out_specs=[vmem()] * 5,
        compiler_params=params(),
        cost_estimate=cost(8 * TOKENS * feat * feat, 7e6),
        name="own",
    )(scal, tok, weight)

    kvh, kvht, nht = pl.pallas_call(
        functools.partial(kernel_halo, bits, len(steps)),
        out_shape=(
            struct((padded, 2 * feat), BF16),
            struct((2 * feat, padded), BF16),
            struct((feat, padded), BF16),
        ),
        in_specs=[smem()] + [vmem()] * (len(steps) + 1),
        out_specs=[vmem()] * 3,
        compiler_params=params(),
        cost_estimate=cost(6 * padded * feat * feat, 2e6),
        name="halo",
    )(scal, *halo_tokens, weight)

    atts, grads, reduced = [], [], []
    prior = None
    ends = np.cumsum([0, *counts])
    for g, heads in enumerate(GROUPS):
        width = len(heads) * HEAD
        last = g == len(GROUPS) - 1
        spans = [(int(a), int(b)) for a, b in zip(ends[:-1], ends[1:])] if last else [(0, padded)]
        out_type = BF16 if last else F32
        outs = pl.pallas_call(
            functools.partial(kernel_attend, heads, g == 0, spans),
            out_shape=(
                *[struct((TOKENS, width), BF16)] * 4,
                struct((feat // 2, 3 * width), F32),
                struct((feat // 2, 3 * width), BF16),
                *[struct((hi - lo, feat), out_type) for lo, hi in spans],
            ),
            in_specs=[vmem()] * (11 if g == 0 else 12),
            out_specs=[vmem()] * (6 + len(spans)),
            scratch_shapes=[
                pltpu.VMEM((TOKENS + padded, 2 * TOKENS), BF16),
                pltpu.VMEM((TOKENS + padded, 2 * TOKENS), BF16),
                pltpu.VMEM((2 * TOKENS, 2 * HEAD), BF16),
                pltpu.VMEM((2 * TOKENS, 2 * HEAD), BF16),
                pltpu.VMEM((width, TOKENS), F32),
                pltpu.VMEM((width, TOKENS), F32),
                pltpu.VMEM((TOKENS + padded, 2 * width), BF16),
            ],
            compiler_params=params(),
            cost_estimate=cost(
                48 * TOKENS * (TOKENS + padded) * width, 6e6, TOKENS * (TOKENS + padded) * len(heads)
            ),
            name=f"attend{g}",
        )(q, kv, kvt, nt, bias, kvh, kvht, nht, hbias, cot, weight, *([] if g == 0 else [prior]))
        atts.append(outs[0])
        grads.extend(outs[1:4])
        keep, send = outs[4], outs[5]
        total = keep + swap(send, "sample", 0).astype(F32)
        for bit in range(bits - 1):
            half = total.shape[0] // 2
            total = total[:half] + swap(total[half:].astype(BF16), "space", bit).astype(F32)
        reduced.append(total)
        prior = outs[6]
        rims = outs[6:]

    arrived = [
        shift(rim, "space", r * grid_cols + c) for (r, c), rim in zip(steps, rims)
    ]
    token_grad = pl.pallas_call(
        functools.partial(kernel_final, len(GROUPS), len(steps)),
        out_shape=struct((TOKENS, feat), BF16),
        in_specs=[vmem()] * (3 + len(grads) + len(steps)),
        out_specs=vmem(),
        compiler_params=params(),
        cost_estimate=cost(6 * TOKENS * feat * feat, 5e6),
        name="final",
    )(tok, weight, jnp.asarray(rim_index), *grads, *arrived)

    pieces = []
    for j in range(3):
        for g, heads in enumerate(GROUPS):
            width = len(heads) * HEAD
            pieces.append(reduced[g][:, j * width : (j + 1) * width])
    total = jnp.concatenate(pieces, axis=1)
    for bit in range((n_sample - 1).bit_length() - 1, 0, -1):
        half = total.shape[1] // 2
        upper = ((member >> bit) & 1) == 1
        mine = jnp.where(upper, total[:, half:], total[:, :half])
        other = jnp.where(upper, total[:, :half], total[:, half:])
        total = mine + swap(other.astype(BF16), "sample", bit).astype(F32)
    half = total.shape[1] // 2
    upper = (member & 1) == 1
    mine = jnp.where(upper, total[:, half:], total[:, :half])
    other = jnp.where(upper, total[:, :half], total[:, half:])
    got = swap(other, "sample", 0)
    weight_grad = jnp.where(
        upper, jnp.concatenate([got, mine], axis=0), jnp.concatenate([mine, got], axis=0)
    )
    attention = jnp.concatenate(atts, axis=1)[None, None]
    return (attention, token_grad[None, None], weight_grad)


def solution(mesh):
    return jax.shard_map(
        local,
        mesh=mesh,
        in_specs=(
            P(("groups", "sample"), "space", None, None),
            P(("groups", "sample"), "space", None, None),
            P("groups", None),
            P(("groups", "sample"), None),
        ),
        out_specs=(
            P(("groups", "sample"), "space", None, None),
            P(("groups", "sample"), "space", None, None),
            P(("groups", "space"), "sample"),
        ),
        check_vma=False,
    )
```

```python
import functools
import math

import jax
import jax.numpy as jnp
import numpy as np
from jax import lax
from jax.experimental import pallas as pl
from jax.experimental.pallas import tpu as pltpu
from jax.sharding import PartitionSpec as P

HEADS = 8
HEAD = 64
TH = 16
TW = 32
HALO = 3
TOKENS = TH * TW
NEG = -1e30
LAST = (((1,), (1,)), ((), ()))
F32 = jnp.float32
BF16 = jnp.bfloat16
CHUNK = 256
ROWS = 64

vmem = functools.partial(pl.BlockSpec, memory_space=pltpu.VMEM)
smem = functools.partial(pl.BlockSpec, memory_space=pltpu.SMEM)


def params():
    return pltpu.CompilerParams(vmem_limit_bytes=24 * 1024 * 1024)


def dot(a, b):
    return jnp.dot(a, b, preferred_element_type=F32)


def dot_t(a, b):
    return lax.dot_general(a, b, LAST, preferred_element_type=F32)


def normalise(tok):
    tok = tok.astype(F32)
    centred = tok - jnp.mean(tok, axis=-1, keepdims=True)
    inv = lax.rsqrt(jnp.mean(centred * centred, axis=-1, keepdims=True) + 1e-05)
    return centred * inv, inv


def own_ids(cols):
    position = lax.axis_index("space")
    member = lax.axis_index("sample")
    return position, member, position // cols, position % cols


def live(row, col, margin_ref, rows, cols):
    return (
        (row >= margin_ref[0, 0])
        & (row < rows - margin_ref[0, 1])
        & (col >= margin_ref[0, 2])
        & (col < cols - margin_ref[0, 3])
    )


def permutation(feat, n_space, position, member):
    bits = (n_space - 1).bit_length()
    size = feat // (4 * n_space)
    row = lax.broadcasted_iota(jnp.int32, (feat, feat), 0)
    col = lax.broadcasted_iota(jnp.int32, (feat, feat), 1)
    relative = row // size
    space = jnp.zeros_like(row)
    for i in range(bits):
        space = space | (((relative >> (bits - 1 - i)) & 1) << i)
    space = space ^ position
    part = (relative >> bits) & 1
    half = (relative >> (bits + 1)) ^ (member & 1)
    source = ((space * 2 + half) * 2 + part) * size + row % size
    return jnp.where(col == source, 1.0, 0.0).astype(BF16)


def kernel_own(sizes, margin_ref, tok_ref, w_ref, q_ref, kv_ref, kvt_ref, nt_ref, bias_ref):
    n_space, grid_cols, plane_rows, plane_cols = sizes
    position, member, tile_row, tile_col = own_ids(grid_cols)
    feat = w_ref.shape[0]
    standard, _ = normalise(tok_ref[...])
    normed = standard.astype(BF16)
    scale = 1.0 / math.sqrt(HEAD)
    q_ref[...] = (dot(normed, w_ref[:, :feat]).astype(BF16).astype(F32) * scale).astype(BF16)
    for i in range(2):
        part = dot(normed, w_ref[:, (i + 1) * feat : (i + 2) * feat]).astype(BF16)
        kv_ref[:TOKENS, i * feat : (i + 1) * feat] = part
        kvt_ref[i * feat : (i + 1) * feat, :TOKENS] = part.T
    nt_ref[:, :TOKENS] = dot_t(permutation(feat, n_space, position, member), normed).astype(BF16)
    key = lax.broadcasted_iota(jnp.int32, (TOKENS, TOKENS), 0)
    query = lax.broadcasted_iota(jnp.int32, (TOKENS, TOKENS), 1)
    row = tile_row * TH + key // TW
    col = tile_col * TW + key % TW
    is_open = live(row, col, margin_ref, plane_rows, plane_cols) | (key == query)
    bias_ref[:TOKENS, :] = jnp.where(is_open, 0.0, NEG)


def kernel_attend(sizes, n_sample, spans, margin_ref, coord_ref, q_ref, cot_ref, w_ref, *refs):
    n_space, grid_cols, plane_rows, plane_cols = sizes
    count = len(spans)
    toks, refs = refs[:count], refs[count + 4 :]
    kv_ref, kvt_ref, nt_ref, bias_ref, att_ref, gq_ref, gkv_ref, keep_ref, send_ref = refs[:9]
    gnh_refs, refs = refs[9 : 9 + count], refs[9 + count :]
    s_s, g_s, pb_s, ds_s, cm_s, qm_s, att_s, dqt_s, gh_s = refs
    position, member, tile_row, tile_col = own_ids(grid_cols)
    feat = w_ref.shape[0]
    keys = kv_ref.shape[0]
    padded = keys - TOKENS
    scale = 1.0 / math.sqrt(HEAD)

    parts = [r[...].astype(F32) for r in toks]
    if spans[-1][1] < padded:
        parts.append(jnp.zeros((padded - spans[-1][1], feat), F32))
    standard, _ = normalise(jnp.concatenate(parts, axis=0))
    normed = standard.astype(BF16)
    for i in range(2):
        part = dot(normed, w_ref[:, (i + 1) * feat : (i + 2) * feat]).astype(BF16)
        kv_ref[TOKENS:, i * feat : (i + 1) * feat] = part
        kvt_ref[i * feat : (i + 1) * feat, TOKENS:] = part.T
    nt_ref[:, TOKENS:] = dot_t(permutation(feat, n_space, position, member), normed).astype(BF16)
    row = tile_row * TH + coord_ref[:, 0:1]
    col = tile_col * TW + coord_ref[:, 1:2]
    is_open = live(row, col, margin_ref, plane_rows, plane_cols) & (coord_ref[:, 2:3] > 0)
    is_open = is_open & (row >= 0) & (row < plane_rows) & (col >= 0) & (col < plane_cols)
    bias_ref[TOKENS:, :] = jnp.broadcast_to(jnp.where(is_open, 0.0, NEG), (padded, TOKENS))

    lane = lax.broadcasted_iota(jnp.int32, (TOKENS, 2 * HEAD), 1)
    step = 0
    for pair in range(HEADS // 2):
        base = pair * 2 * HEAD
        cols = slice(base, base + 2 * HEAD)
        vcols = slice(feat + base, feat + base + 2 * HEAD)
        q = q_ref[:, cols]
        cot = cot_ref[:, cols]
        zero = jnp.zeros_like(q)
        for odd in range(2):
            mine = (lane >= HEAD) if odd else (lane < HEAD)
            qm_s[odd * TOKENS : (odd + 1) * TOKENS, :] = jnp.where(mine, q, zero)
            cm_s[odd * TOKENS : (odd + 1) * TOKENS, :] = jnp.where(mine, cot, zero)
            krow = base + odd * HEAD
            vrow = feat + krow
            for c in range(TOKENS // CHUNK):
                slot = step % 2
                step += 1
                lanes = slice(c * CHUNK, (c + 1) * CHUNK)
                out = slice(odd * TOKENS + c * CHUNK, odd * TOKENS + (c + 1) * CHUNK)
                s_s[slot] = dot_t(kv_ref[:, cols], qm_s[out, :])
                g_s[slot] = dot_t(kv_ref[:, vcols], cm_s[out, :])
                top = jnp.full((8, CHUNK), NEG, F32)
                for r in range(0, keys, ROWS):
                    x = s_s[slot, r : r + ROWS, :] + bias_ref[r : r + ROWS, lanes]
                    top = jnp.maximum(top, jnp.max(x.reshape(ROWS // 8, 8, CHUNK), axis=0))
                top = jnp.max(top, axis=0, keepdims=True)
                total = jnp.zeros((8, CHUNK), F32)
                delta = jnp.zeros((8, CHUNK), F32)
                for r in range(0, keys, ROWS):
                    x = s_s[slot, r : r + ROWS, :] + bias_ref[r : r + ROWS, lanes]
                    e = jnp.exp(x - top)
                    s_s[slot, r : r + ROWS, :] = e
                    total = total + jnp.sum(e.reshape(ROWS // 8, 8, CHUNK), axis=0)
                    eg = e * g_s[slot, r : r + ROWS, :]
                    delta = delta + jnp.sum(eg.reshape(ROWS // 8, 8, CHUNK), axis=0)
                inv = 1.0 / jnp.sum(total, axis=0, keepdims=True)
                delta = jnp.sum(delta, axis=0, keepdims=True) * inv
                for r in range(0, keys, ROWS):
                    p = s_s[slot, r : r + ROWS, :] * inv
                    pb_s[r : r + ROWS, out] = p.astype(BF16)
                    ds_s[r : r + ROWS, out] = (p * (g_s[slot, r : r + ROWS, :] - delta)).astype(BF16)
                att_s[krow : krow + HEAD, lanes] = dot(kvt_ref[vrow : vrow + HEAD, :], pb_s[:, out])
                dqt_s[krow : krow + HEAD, lanes] = scale * dot(kvt_ref[krow : krow + HEAD, :], ds_s[:, out])
        for source, other, at in ((ds_s, qm_s, base), (pb_s, cm_s, feat + base)):
            grad = dot(source[...], other[...]).astype(BF16)
            gkv_ref[:, at : at + 2 * HEAD] = grad[:TOKENS]
            gh_s[:, at : at + 2 * HEAD] = grad[TOKENS:]

    block = 3 * feat // n_sample

    def store(value, at):
        for i in range(0, value.shape[1], 128):
            b, rest = (at + i) // block, (at + i) % block
            mine = pl.multiple_of((b ^ member) * block + rest, 128)
            theirs = pl.multiple_of((b ^ member ^ 1) * block + rest, 128)
            keep_ref[:, pl.ds(mine, 128)] = value[: feat // 2, i : i + 128]
            send_ref[:, pl.ds(theirs, 128)] = value[feat // 2 :, i : i + 128].astype(BF16)

    wide = 256
    for i in range(0, feat, wide):
        store(dot_t(nt_ref[:, :TOKENS], dqt_s[i : i + wide, :].astype(BF16)), i)
    for i in range(0, 2 * feat, wide):
        store(
            dot(nt_ref[:, :TOKENS], gkv_ref[:, i : i + wide]) + dot(nt_ref[:, TOKENS:], gh_s[:, i : i + wide]),
            feat + i,
        )
    gnh = dot_t(gh_s[...], w_ref[:, feat:])
    for (lo, hi), ref in zip(spans, gnh_refs):
        ref[...] = gnh[lo:hi, :].astype(BF16)
    gq_ref[...] = dqt_s[...].T.astype(BF16)
    att_ref[...] = att_s[...].T.astype(BF16)


def kernel_final(count, tok_ref, w_ref, index_ref, gq_ref, gkv_ref, *refs):
    arrived, out_ref = refs[:count], refs[count]
    feat = w_ref.shape[0]
    total = dot_t(gq_ref[...], w_ref[:, :feat]) + dot_t(gkv_ref[...], w_ref[:, feat:])
    padded = index_ref.shape[1]
    parts = [r[...].astype(F32) for r in arrived]
    have = sum(p.shape[0] for p in parts)
    if have < padded:
        parts.append(jnp.zeros((padded - have, feat), F32))
    rim = jnp.concatenate(parts, axis=0).astype(BF16)
    token = lax.broadcasted_iota(jnp.int32, (TOKENS, padded), 0)
    place = jnp.where(token == index_ref[...], 1.0, 0.0).astype(BF16)
    total = total + dot(place, rim)
    standard, inv = normalise(tok_ref[...])
    mean = jnp.mean(total, axis=-1, keepdims=True)
    cross = jnp.mean(total * standard, axis=-1, keepdims=True)
    out_ref[...] = ((total - mean - standard * cross) * inv).astype(BF16)


def shift(value, axis, steps):
    count = lax.axis_size(axis)
    first, last = max(0, -steps), min(count, count - steps)
    return lax.ppermute(value, axis, [(i, i + steps) for i in range(first, last)])


def swap(value, axis, bit):
    count = lax.axis_size(axis)
    return lax.ppermute(value, axis, [(i, i ^ (1 << bit)) for i in range(count)])


def span(step, length):
    if step < 0:
        return (length - HALO, length)
    if step > 0:
        return (0, HALO)
    return (0, length)


def window_span(step, length):
    if step < 0:
        return (-HALO, 0)
    if step > 0:
        return (length, length + HALO)
    return (0, length)


def struct(shape, dtype):
    return jax.ShapeDtypeStruct(shape, dtype)


def cost(flops, nbytes, exps=0):
    return pl.CostEstimate(flops=int(flops), bytes_accessed=int(nbytes), transcendentals=int(exps))


def halve(keep, send, axis, bit):
    return keep + swap(send.astype(BF16), axis, bit).astype(F32)


def local(tokens, cotangent, weight, margins):
    feat = weight.shape[0]
    tok, cot = tokens[0, 0], cotangent[0, 0]
    n_space, n_sample = lax.axis_size("space"), lax.axis_size("sample")
    grid_cols = min(8, n_space)
    grid_rows = n_space // grid_cols
    sizes = (n_space, grid_cols, grid_rows * TH, grid_cols * TW)
    member = lax.axis_index("sample")
    row_steps = (-1, 0, 1) if grid_rows > 1 else (0,)
    steps = [(r, c) for r in row_steps for c in (-1, 0, 1) if (r, c) != (0, 0)]
    counts, coords, sources = [], [], []
    for r, c in steps:
        rr, cc = np.meshgrid(
            np.arange(*window_span(r, TH)), np.arange(*window_span(c, TW)), indexing="ij"
        )
        coords.append(np.stack([rr.ravel(), cc.ravel(), np.ones(rr.size, np.int64)], axis=1))
        rr, cc = np.meshgrid(np.arange(*span(r, TH)), np.arange(*span(c, TW)), indexing="ij")
        sources.append((rr * TW + cc).ravel())
        counts.append(rr.size)
    halo = sum(counts)
    padded = -(-halo // 128) * 128
    keys = TOKENS + padded
    coords = np.concatenate([*coords, np.zeros((padded - halo, 3), np.int64)]).astype(np.int32)
    rim_index = np.concatenate([*sources, np.full(padded - halo, -1)]).astype(np.int32)[None, :]
    ends = np.cumsum([0, *counts])
    spans = [(int(a), int(b)) for a, b in zip(ends[:-1], ends[1:])]

    grid = tok.reshape(TH, TW, feat)
    halo_tokens = []
    for (r, c), n in zip(steps, counts):
        (r0, r1), (c0, c1) = span(r, TH), span(c, TW)
        piece = grid[r0:r1, c0:c1].reshape(n, feat)
        halo_tokens.append(shift(piece, "space", -(r * grid_cols + c)))

    q, *window = pl.pallas_call(
        functools.partial(kernel_own, sizes),
        out_shape=(
            struct((TOKENS, feat), BF16),
            struct((keys, 2 * feat), BF16),
            struct((2 * feat, keys), BF16),
            struct((feat, keys), BF16),
            struct((keys, TOKENS), F32),
        ),
        in_specs=[smem(), vmem(), vmem()],
        out_specs=[vmem()] * 5,
        compiler_params=params(),
        cost_estimate=cost(8 * TOKENS * feat * feat, 7e6),
        name="own",
    )(margins, tok, weight)

    outs = pl.pallas_call(
        functools.partial(kernel_attend, sizes, n_sample, spans),
        out_shape=(
            *[struct(a.shape, a.dtype) for a in window],
            struct((TOKENS, feat), BF16),
            struct((TOKENS, feat), BF16),
            struct((TOKENS, 2 * feat), BF16),
            struct((feat // 2, 3 * feat), F32),
            struct((feat // 2, 3 * feat), BF16),
            *[struct((n, feat), BF16) for n in counts],
        ),
        in_specs=[smem()] + [vmem()] * (4 + len(counts) + 4),
        out_specs=[vmem()] * (9 + len(counts)),
        input_output_aliases={5 + len(counts) + i: i for i in range(4)},
        scratch_shapes=[
            pltpu.VMEM((2, keys, CHUNK), F32),
            pltpu.VMEM((2, keys, CHUNK), F32),
            pltpu.VMEM((keys, 2 * TOKENS), BF16),
            pltpu.VMEM((keys, 2 * TOKENS), BF16),
            pltpu.VMEM((2 * TOKENS, 2 * HEAD), BF16),
            pltpu.VMEM((2 * TOKENS, 2 * HEAD), BF16),
            pltpu.VMEM((feat, TOKENS), F32),
            pltpu.VMEM((feat, TOKENS), F32),
            pltpu.VMEM((padded, 2 * feat), BF16),
        ],
        compiler_params=params(),
        cost_estimate=cost(48 * TOKENS * keys * feat, 6e6, TOKENS * keys * HEADS),
        name="attend",
    )(margins, jnp.asarray(coords), q, cot, weight, *halo_tokens, *window)
    attention, gq, gkv, keep, send = outs[4:9]
    rims = outs[9:]

    arrived = [shift(rim, "space", r * grid_cols + c) for (r, c), rim in zip(steps, rims)]

    total = keep + swap(send, "sample", 0).astype(F32)
    half = total.shape[0] // 2
    first, second = total[:half], total[half:]
    row_bits = range((n_space - 1).bit_length())
    col_bits = range((n_sample - 1).bit_length() - 1, 0, -1)

    def by_cols(value):
        for bit in col_bits:
            n = value.shape[1] // 2
            value = halve(value[:, :n], value[:, n:], "sample", bit)
        return value

    def by_rows(value):
        for bit in row_bits:
            n = value.shape[0] // 2
            value = halve(value[:n], value[n:], "space", bit)
        return value

    total = jnp.concatenate([by_rows(by_cols(first)), by_cols(by_rows(second))], axis=0)
    n = total.shape[1] // 2
    mine, got = total[:, :n], swap(total[:, n:], "sample", 0)
    weight_grad = jnp.where(
        (member & 1) == 1, jnp.concatenate([got, mine], axis=0), jnp.concatenate([mine, got], axis=0)
    )

    token_grad = pl.pallas_call(
        functools.partial(kernel_final, len(steps)),
        out_shape=struct((TOKENS, feat), BF16),
        in_specs=[vmem()] * (5 + len(steps)),
        out_specs=vmem(),
        compiler_params=params(),
        cost_estimate=cost(6 * TOKENS * feat * feat, 5e6),
        name="final",
    )(tok, weight, jnp.asarray(rim_index), gq, gkv, *arrived)
    return (attention[None, None], token_grad[None, None], weight_grad)


def solution(mesh):
    return jax.shard_map(
        local,
        mesh=mesh,
        in_specs=(
            P(("groups", "sample"), "space", None, None),
            P(("groups", "sample"), "space", None, None),
            P("groups", None),
            P(("groups", "sample"), None),
        ),
        out_specs=(
            P(("groups", "sample"), "space", None, None),
            P(("groups", "sample"), "space", None, None),
            P(("groups", "space"), "sample"),
        ),
        check_vma=False,
    )
```

```python
import functools
import math

import jax
import jax.numpy as jnp
import numpy as np
from jax import lax
from jax.experimental import pallas as pl
from jax.experimental.pallas import tpu as pltpu
from jax.sharding import PartitionSpec as P

HEADS = 8
HEAD = 64
TH = 16
TW = 32
HALO = 3
TOKENS = TH * TW
NEG = -1e30
LAST = (((1,), (1,)), ((), ()))
F32 = jnp.float32
BF16 = jnp.bfloat16
CHUNK = 512
ROWS = 64

vmem = functools.partial(pl.BlockSpec, memory_space=pltpu.VMEM)
hbm = functools.partial(pl.BlockSpec, memory_space=pltpu.HBM)


def params():
    return pltpu.CompilerParams(vmem_limit_bytes=24 * 1024 * 1024)


def dot(a, b):
    return jnp.dot(a, b, preferred_element_type=F32)


def dot_t(a, b):
    return lax.dot_general(a, b, LAST, preferred_element_type=F32)


def normalise(tok):
    tok = tok.astype(F32)
    centred = tok - jnp.mean(tok, axis=-1, keepdims=True)
    inv = lax.rsqrt(jnp.mean(centred * centred, axis=-1, keepdims=True) + 1e-05)
    return centred * inv, inv


def own_ids(cols):
    position = lax.axis_index("space")
    member = lax.axis_index("sample")
    return position, member, position // cols, position % cols


def live(row, col, margin_ref, rows, cols):
    return (
        (row >= margin_ref[0, 0])
        & (row < rows - margin_ref[0, 1])
        & (col >= margin_ref[0, 2])
        & (col < cols - margin_ref[0, 3])
    )


def row_masks(sizes):
    bits = (sizes[0] - 1).bit_length()
    one_row = sizes[1] == sizes[0]
    return [((2 << i) - 1) if one_row else (1 << i) for i in range(bits)]


def paired(sizes):
    return sizes[1] == sizes[0] and sizes[0] in (2, 4)


def permutation(feat, sizes, position):
    masks = row_masks(sizes)
    bits = len(masks)
    size = feat // (2 * sizes[0])
    row = lax.broadcasted_iota(jnp.int32, (feat, feat), 0)
    col = lax.broadcasted_iota(jnp.int32, (feat, feat), 1)
    relative = row // size
    space = jnp.zeros_like(row) + position
    for i, mask in enumerate(masks):
        space = space ^ (((relative >> (bits - 1 - i)) & 1) * mask)
    part = (relative >> bits) & 1
    source = (space * 2 + part) * size + row % size
    return jnp.where(col == source, 1.0, 0.0).astype(BF16)


def kernel_own(
    sizes, pieces, margin_hbm, tok_hbm, w_hbm, q_ref, kv_ref, kvt_ref, nt_ref, bias_ref, margin_ref, tok_s, w_s, sems
):
    n_space, grid_cols, plane_rows, plane_cols = sizes
    feat = w_hbm.shape[0]
    copies = [pltpu.make_async_copy(tok_hbm, tok_s, sems.at[0])]
    for i in range(3):
        cols = pl.ds(i * feat, feat)
        copies.append(pltpu.make_async_copy(w_hbm.at[:, cols], w_s.at[:, cols], sems.at[1 + i]))
    copies.append(pltpu.make_async_copy(margin_hbm, margin_ref, sems.at[4]))
    for copy in copies:
        copy.start()
    position, member, tile_row, tile_col = own_ids(grid_cols)
    copies[4].wait()
    key = lax.broadcasted_iota(jnp.int32, (TOKENS, TOKENS), 0)
    query = lax.broadcasted_iota(jnp.int32, (TOKENS, TOKENS), 1)
    row = tile_row * TH + key // TW
    col = tile_col * TW + key % TW
    is_open = live(row, col, margin_ref, plane_rows, plane_cols) | (key == query)
    bias_ref[:TOKENS, :] = jnp.where(is_open, 0.0, NEG)
    padded = bias_ref.shape[0] - TOKENS
    index = lax.broadcasted_iota(jnp.int32, (padded, TOKENS), 0)
    row = jnp.full((padded, TOKENS), -1, jnp.int32)
    col = row
    for start, count, r0, c0, wide in pieces:
        at = index - start
        down = (at * 171) >> 9 if wide == 3 else at // wide
        here = (at >= 0) & (at < count)
        row = jnp.where(here, tile_row * TH + r0 + down, row)
        col = jnp.where(here, tile_col * TW + c0 + at - down * wide, col)
    is_open = live(row, col, margin_ref, plane_rows, plane_cols)
    is_open = is_open & (row >= 0) & (row < plane_rows) & (col >= 0) & (col < plane_cols)
    bias_ref[TOKENS:, :] = jnp.where(is_open, 0.0, NEG)
    place = permutation(feat, sizes, position)
    copies[0].wait()
    standard, _ = normalise(tok_s[...])
    normed = standard.astype(BF16)
    nt_ref[:, :TOKENS] = dot_t(place, normed).astype(BF16)
    scale = 1.0 / math.sqrt(HEAD)
    copies[1].wait()
    q_ref[...] = (dot(normed, w_s[:, :feat]).astype(BF16).astype(F32) * scale).astype(BF16)
    for i in range(2):
        copies[2 + i].wait()
        part = dot(normed, w_s[:, (i + 1) * feat : (i + 2) * feat]).astype(BF16)
        kv_ref[:TOKENS, i * feat : (i + 1) * feat] = part
        kvt_ref[i * feat : (i + 1) * feat, :TOKENS] = part.T


def kernel_attend(sizes, n_sample, spans, q_ref, cot_ref, w_ref, bias_ref, *refs):
    n_space, grid_cols, plane_rows, plane_cols = sizes
    count = len(spans)
    toks, refs = refs[:count], refs[count + 3 :]
    kv_ref, kvt_ref, nt_ref, att_ref, grad_ref, keep_ref, send_ref = refs[:7]
    rim_refs, refs = refs[7 : 7 + count], refs[7 + count :]
    s_s, g_s, pb_s, ds_s, cm_s, qm_s, att_s, dqt_s = refs
    position, member, tile_row, tile_col = own_ids(grid_cols)
    feat = w_ref.shape[0]
    keys = kv_ref.shape[0]
    padded = keys - TOKENS
    scale = 1.0 / math.sqrt(HEAD)

    parts = [r[...].astype(F32) for r in toks]
    even = (position & 1) == 0
    if paired(sizes):
        parts = [jnp.where(even, parts[1], parts[0]), jnp.where(even, parts[0], parts[1])]
    if spans[-1][1] < padded:
        parts.append(jnp.zeros((padded - spans[-1][1], feat), F32))
    standard, _ = normalise(jnp.concatenate(parts, axis=0))
    normed = standard.astype(BF16)
    for i in range(2):
        part = dot(normed, w_ref[:, (i + 1) * feat : (i + 2) * feat]).astype(BF16)
        kv_ref[TOKENS:, i * feat : (i + 1) * feat] = part
        kvt_ref[i * feat : (i + 1) * feat, TOKENS:] = part.T
    nt_ref[:, TOKENS:] = dot_t(permutation(feat, sizes, position), normed).astype(BF16)
    lane = lax.broadcasted_iota(jnp.int32, (TOKENS, 2 * HEAD), 1)
    step = 0
    for pair in range(HEADS // 2):
        base = pair * 2 * HEAD
        cols = slice(base, base + 2 * HEAD)
        vcols = slice(feat + base, feat + base + 2 * HEAD)
        q = q_ref[:, cols]
        cot = cot_ref[:, cols]
        zero = jnp.zeros_like(q)
        for odd in range(2):
            mine = (lane >= HEAD) if odd else (lane < HEAD)
            qm_s[odd * TOKENS : (odd + 1) * TOKENS, :] = jnp.where(mine, q, zero)
            cm_s[odd * TOKENS : (odd + 1) * TOKENS, :] = jnp.where(mine, cot, zero)
            krow = base + odd * HEAD
            vrow = feat + krow
            for c in range(TOKENS // CHUNK):
                slot = step % 2
                step += 1
                lanes = slice(c * CHUNK, (c + 1) * CHUNK)
                out = slice(odd * TOKENS + c * CHUNK, odd * TOKENS + (c + 1) * CHUNK)
                s_s[slot] = dot_t(kv_ref[:, cols], qm_s[out, :])
                g_s[slot] = dot_t(kv_ref[:, vcols], cm_s[out, :])
                top = jnp.full((8, CHUNK), NEG, F32)
                for r in range(0, keys, ROWS):
                    x = s_s[slot, r : r + ROWS, :] + bias_ref[r : r + ROWS, lanes]
                    top = jnp.maximum(top, jnp.max(x.reshape(ROWS // 8, 8, CHUNK), axis=0))
                top = jnp.max(top, axis=0, keepdims=True)
                total = jnp.zeros((8, CHUNK), F32)
                delta = jnp.zeros((8, CHUNK), F32)
                for r in range(0, keys, ROWS):
                    x = s_s[slot, r : r + ROWS, :] + bias_ref[r : r + ROWS, lanes]
                    e = jnp.exp(x - top)
                    s_s[slot, r : r + ROWS, :] = e
                    total = total + jnp.sum(e.reshape(ROWS // 8, 8, CHUNK), axis=0)
                    eg = e * g_s[slot, r : r + ROWS, :]
                    delta = delta + jnp.sum(eg.reshape(ROWS // 8, 8, CHUNK), axis=0)
                inv = 1.0 / jnp.sum(total, axis=0, keepdims=True)
                delta = jnp.sum(delta, axis=0, keepdims=True) * inv
                for r in range(0, keys, ROWS):
                    p = s_s[slot, r : r + ROWS, :] * inv
                    pb_s[r : r + ROWS, out] = p.astype(BF16)
                    ds_s[r : r + ROWS, out] = (p * (g_s[slot, r : r + ROWS, :] - delta)).astype(BF16)
                att_s[krow : krow + HEAD, lanes] = dot(kvt_ref[vrow : vrow + HEAD, :], pb_s[:, out])
                dqt_s[krow : krow + HEAD, lanes] = scale * dot(kvt_ref[krow : krow + HEAD, :], ds_s[:, out])
        for source, other, at in ((ds_s, qm_s, feat + base), (pb_s, cm_s, 2 * feat + base)):
            grad_ref[:, at : at + 2 * HEAD] = dot(source[...], other[...]).astype(BF16)
    grad_ref[:TOKENS, :feat] = dqt_s[...].T.astype(BF16)
    grad_ref[TOKENS:, :feat] = jnp.zeros((padded, feat), BF16)

    block = 3 * feat // n_sample
    for j in range(n_sample // 2):
        for target, other in ((keep_ref, 2 * j), (send_ref, 2 * j + 1)):
            cols = pl.ds(pl.multiple_of((member ^ other) * block, 128), block)
            value = dot(nt_ref[...], grad_ref[:, cols])
            target[:, j * block : (j + 1) * block] = value.astype(target.dtype)
    rim = dot_t(grad_ref[TOKENS:, feat:], w_ref[:, feat:])
    if paired(sizes):
        rows = rim_refs[0].shape[0]
        left, right = (rim[lo:hi, :] for lo, hi in spans)
        for ref, value in zip(rim_refs, (jnp.where(even, right, left), jnp.where(even, left, right))):
            wide = feat // 2
            value = jnp.concatenate([value[:, :wide], value[:, wide:]], axis=0).astype(BF16)
            for i in range(3):
                ref[:, i * wide : (i + 1) * wide] = value[i * rows : (i + 1) * rows]
    else:
        for (lo, hi), ref in zip(spans, rim_refs):
            ref[...] = rim[lo:hi, :].astype(BF16)
    att_ref[...] = att_s[...].T.astype(BF16)


def kernel_final(sizes, count, tok_ref, w_ref, index_ref, grad_ref, *refs):
    arrived, out_ref = refs[:count], refs[count]
    feat = w_ref.shape[0]
    total = dot_t(grad_ref[:TOKENS, :], w_ref[...])
    padded = index_ref.shape[1]
    parts = [r[...].astype(F32) for r in arrived]
    if paired(sizes):
        even = (lax.axis_index("space") & 1) == 0
        wide = feat // 2
        parts = [jnp.concatenate([p[:, i * wide : (i + 1) * wide] for i in range(3)], axis=0) for p in parts]
        parts = [jnp.concatenate([p[: p.shape[0] // 2], p[p.shape[0] // 2 :]], axis=1) for p in parts]
        parts = [jnp.where(even, parts[1], parts[0]), jnp.where(even, parts[0], parts[1])]
    have = sum(p.shape[0] for p in parts)
    if have < padded:
        parts.append(jnp.zeros((padded - have, feat), F32))
    rim = jnp.concatenate(parts, axis=0).astype(BF16)
    token = lax.broadcasted_iota(jnp.int32, (TOKENS, padded), 0)
    place = jnp.where(token == index_ref[...], 1.0, 0.0).astype(BF16)
    total = total + dot(place, rim)
    standard, inv = normalise(tok_ref[...])
    mean = jnp.mean(total, axis=-1, keepdims=True)
    cross = jnp.mean(total * standard, axis=-1, keepdims=True)
    out_ref[...] = ((total - mean - standard * cross) * inv).astype(BF16)


def shift(value, axis, steps):
    count = lax.axis_size(axis)
    first, last = max(0, -steps), min(count, count - steps)
    return lax.ppermute(value, axis, [(i, i + steps) for i in range(first, last)])


def span(step, length):
    if step < 0:
        return (length - HALO, length)
    if step > 0:
        return (0, HALO)
    return (0, length)


def window_span(step, length):
    if step < 0:
        return (-HALO, 0)
    if step > 0:
        return (length, length + HALO)
    return (0, length)


def struct(shape, dtype):
    return jax.ShapeDtypeStruct(shape, dtype)


def cost(flops, nbytes, exps=0):
    return pl.CostEstimate(flops=int(flops), bytes_accessed=int(nbytes), transcendentals=int(exps))


def exchange(value, axis, mask):
    count = lax.axis_size(axis)
    return lax.ppermute(value, axis, [(i, i ^ mask) for i in range(count)])


def local(tokens, cotangent, weight, margins):
    feat = weight.shape[0]
    tok, cot = tokens[0, 0], cotangent[0, 0]
    n_space, n_sample = lax.axis_size("space"), lax.axis_size("sample")
    grid_cols = min(8, n_space)
    grid_rows = n_space // grid_cols
    sizes = (n_space, grid_cols, grid_rows * TH, grid_cols * TW)
    masks = row_masks(sizes)
    row_steps = (-1, 0, 1) if grid_rows > 1 else (0,)
    steps = [(r, c) for r in row_steps for c in (-1, 0, 1) if (r, c) != (0, 0)]
    counts, pieces, sources = [], [], []
    way = -1 if paired(sizes) else 1
    for r, c in steps:
        (r0, r1), (c0, c1) = window_span(r, TH), window_span(c, TW)
        pieces.append((sum(counts), (r1 - r0) * (c1 - c0), r0, c0, c1 - c0))
        rr, cc = np.meshgrid(np.arange(*span(way * r, TH)), np.arange(*span(way * c, TW)), indexing="ij")
        sources.append((rr * TW + cc).ravel())
        counts.append(pieces[-1][1])
    halo = sum(counts)
    padded = -(-halo // 128) * 128
    keys = TOKENS + padded
    rim_index = np.concatenate([*sources, np.full(padded - halo, -1)]).astype(np.int32)[None, :]
    ends = np.cumsum([0, *counts])
    spans = [(int(a), int(b)) for a, b in zip(ends[:-1], ends[1:])]

    grid = tok.reshape(TH, TW, feat)
    even = (lax.axis_index("space") & 1) == 0
    rims = []
    for r, c in steps:
        (r0, r1), (c0, c1) = span(r, TH), span(c, TW)
        rims.append(grid[r0:r1, c0:c1].reshape(-1, feat))
    if paired(sizes):
        sent = (jnp.where(even, rims[0], rims[1]), jnp.where(even, rims[1], rims[0]))
        halo_tokens = [exchange(v, "space", m) for v, m in zip(sent, masks)]
        halo_tokens += [jnp.zeros_like(rims[0])] * (2 - len(masks))
    else:
        halo_tokens = [shift(v, "space", -(r * grid_cols + c)) for v, (r, c) in zip(rims, steps)]

    q, kv, kvt, nt, bias = pl.pallas_call(
        functools.partial(kernel_own, sizes, pieces),
        out_shape=(
            struct((TOKENS, feat), BF16),
            struct((keys, 2 * feat), BF16),
            struct((2 * feat, keys), BF16),
            struct((feat, keys), BF16),
            struct((keys, TOKENS), F32),
        ),
        in_specs=[hbm()] * 3,
        out_specs=[vmem()] * 5,
        scratch_shapes=[
            pltpu.SMEM(margins.shape, jnp.int32),
            pltpu.VMEM(tok.shape, BF16),
            pltpu.VMEM(weight.shape, BF16),
            pltpu.SemaphoreType.DMA((5,)),
        ],
        compiler_params=params(),
        cost_estimate=cost(8 * TOKENS * feat * feat, 7e6),
        name="own",
    )(margins, tok, weight)

    rim_shape = (2 * counts[0] // 3, 3 * feat // 2)
    outs = pl.pallas_call(
        functools.partial(kernel_attend, sizes, n_sample, spans),
        out_shape=(
            *[struct(a.shape, a.dtype) for a in (kv, kvt, nt)],
            struct((TOKENS, feat), BF16),
            struct((keys, 3 * feat), BF16),
            struct((feat, 3 * feat // 2), F32),
            struct((feat, 3 * feat // 2), BF16),
            *[struct(rim_shape if paired(sizes) else (n, feat), BF16) for n in counts],
        ),
        in_specs=[vmem()] * (4 + len(counts) + 3),
        out_specs=[vmem()] * (7 + len(counts)),
        input_output_aliases={4 + len(counts) + i: i for i in range(3)},
        scratch_shapes=[
            pltpu.VMEM((2, keys, CHUNK), F32),
            pltpu.VMEM((2, keys, CHUNK), F32),
            pltpu.VMEM((keys, 2 * TOKENS), BF16),
            pltpu.VMEM((keys, 2 * TOKENS), BF16),
            pltpu.VMEM((2 * TOKENS, 2 * HEAD), BF16),
            pltpu.VMEM((2 * TOKENS, 2 * HEAD), BF16),
            pltpu.VMEM((feat, TOKENS), F32),
            pltpu.VMEM((feat, TOKENS), F32),
        ],
        compiler_params=params(),
        cost_estimate=cost(48 * TOKENS * keys * feat, 6e6, TOKENS * keys * HEADS),
        name="attend",
    )(q, cot, weight, bias, *halo_tokens, kv, kvt, nt)
    attention, grads, keep, send = outs[3:7]
    rims = list(outs[7:])

    total = keep + exchange(send, "sample", 1).astype(F32)
    half = feat // 2
    first, second = total[:half], total[half:]
    col_masks = [1 << bit for bit in range((n_sample - 1).bit_length() - 1, 0, -1)]
    arrived = []
    if not paired(sizes):
        arrived = [shift(rim, "space", r * grid_cols + c) for (r, c), rim in zip(steps, rims)]

    def by_cols(value):
        for mask in col_masks:
            n = value.shape[1] // 2
            got = exchange(value[:, n:].astype(BF16), "sample", mask)
            value = value[:, :n] + got.astype(F32)
        return value

    def by_rows(value, riders):
        for i, mask in enumerate(masks):
            n = value.shape[0] // 2
            out = value[n:].astype(BF16)
            if riders:
                out = jnp.concatenate([out, riders[i]], axis=0)
            got = exchange(out, "space", mask)
            if riders:
                arrived.append(got[n:])
            value = value[:n] + got[:n].astype(F32)
        return value

    upper = by_rows(by_cols(first), [])
    lower = by_cols(by_rows(second, rims if paired(sizes) else []))
    weight_grad = jnp.concatenate([upper, lower], axis=0)
    arrived += [jnp.zeros_like(rim) for rim in rims[len(arrived) :]]

    token_grad = pl.pallas_call(
        functools.partial(kernel_final, sizes, len(steps)),
        out_shape=struct((TOKENS, feat), BF16),
        in_specs=[vmem()] * (4 + len(steps)),
        out_specs=vmem(),
        compiler_params=params(),
        cost_estimate=cost(6 * TOKENS * feat * feat, 5e6),
        name="final",
    )(tok, weight, jnp.asarray(rim_index), grads, *arrived)
    return (attention[None, None], token_grad[None, None], weight_grad)


def solution(mesh):
    return jax.shard_map(
        local,
        mesh=mesh,
        in_specs=(
            P(("groups", "sample"), "space", None, None),
            P(("groups", "sample"), "space", None, None),
            P("groups", None),
            P(("groups", "sample"), None),
        ),
        out_specs=(
            P(("groups", "sample"), "space", None, None),
            P(("groups", "sample"), "space", None, None),
            P(("groups", "space"), "sample"),
        ),
        check_vma=False,
    )
```

```python
import functools
import math

import jax
import jax.numpy as jnp
import numpy as np
from jax import lax
from jax.experimental import pallas as pl
from jax.experimental.pallas import tpu as pltpu
from jax.sharding import PartitionSpec as P

HEADS = 8
HEAD = 64
TH = 16
TW = 32
HALO = 3
TOKENS = TH * TW
NEG = -1e30
LAST = (((1,), (1,)), ((), ()))
F32 = jnp.float32
BF16 = jnp.bfloat16
PACK = 1e6
OWN = 24
ROWS = 64

vmem = functools.partial(pl.BlockSpec, memory_space=pltpu.VMEM)
hbm = functools.partial(pl.BlockSpec, memory_space=pltpu.HBM)


def params(mib=24):
    return pltpu.CompilerParams(vmem_limit_bytes=mib * 1024 * 1024)


def dot(a, b):
    return jnp.dot(a, b, preferred_element_type=F32)


def dot_t(a, b):
    return lax.dot_general(a, b, LAST, preferred_element_type=F32)


def normalise(tok):
    tok = tok.astype(F32)
    centred = tok - jnp.mean(tok, axis=-1, keepdims=True)
    inv = lax.rsqrt(jnp.mean(centred * centred, axis=-1, keepdims=True) + 1e-05)
    return centred * inv, inv


def own_ids(cols):
    position = lax.axis_index("space")
    member = lax.axis_index("sample")
    return position, member, position // cols, position % cols


def live(row, col, margin_ref, rows, cols):
    return (
        (row >= margin_ref[0, 0])
        & (row < rows - margin_ref[0, 1])
        & (col >= margin_ref[0, 2])
        & (col < cols - margin_ref[0, 3])
    )


def row_masks(sizes):
    bits = (sizes[0] - 1).bit_length()
    one_row = sizes[1] == sizes[0]
    return [((2 << i) - 1) if one_row else (1 << i) for i in range(bits)]


def paired(sizes):
    return sizes[1] == sizes[0] and sizes[0] in (2, 4)


def row_split(feat, n_space):
    size = feat // n_space
    return size * 5 // 8 // 16 * 16 if size >= 64 else size // 2


def permutation(feat, sizes, position):
    masks = row_masks(sizes)
    size = feat // sizes[0]
    upper = row_split(feat, sizes[0])
    row = lax.broadcasted_iota(jnp.int32, (feat, 128), 0)
    below = row >= upper * sizes[0]
    at = jnp.where(below, row - upper * sizes[0], row)
    relative = jnp.where(below, at // (size - upper), at // upper)
    rest = at - relative * jnp.where(below, size - upper, upper)
    space = jnp.zeros_like(row) + position
    for i, mask in enumerate(masks):
        space = space ^ (((relative >> (len(masks) - 1 - i)) & 1) * mask)
    source = space * size + jnp.where(below, upper, 0) + rest
    col = lax.broadcasted_iota(jnp.int32, (feat, 128), 1)
    return jnp.concatenate(
        [jnp.where(col + i == source, 1.0, 0.0).astype(BF16) for i in range(0, feat, 128)], axis=1
    )


def kernel_pack(sizes, pieces, tok_hbm, *refs):
    rim_refs, (tok_ref, sem) = refs[: len(pieces)], refs[len(pieces) :]
    copy = pltpu.make_async_copy(tok_hbm, tok_ref, sem)
    copy.start()
    even = (lax.axis_index("space") & 1) == 0
    total = sum(p[1] for p in pieces)
    rows = -(-total // 16) * 16
    index = lax.broadcasted_iota(jnp.int32, (rows, TOKENS), 0)
    token = lax.broadcasted_iota(jnp.int32, (rows, TOKENS), 1)
    wanted = jnp.full((rows, TOKENS), -1, jnp.int32)
    for i, (start, count, _, _, wide, r0, c0) in enumerate(pieces):
        at = index - start
        down = (at * 171) >> 9 if wide == 3 else at // wide
        source = (r0 + down) * TW + c0 + at - down * wide
        if paired(sizes):
            source = source + jnp.where(even, 0, pieces[1 - i][6] - c0)
        wanted = jnp.where((at >= 0) & (at < count), source, wanted)
    select = jnp.where(wanted == token, 1.0, 0.0).astype(BF16)
    copy.wait()
    rims = dot(select, tok_ref[...])
    for (start, count, *_), ref in zip(pieces, rim_refs):
        ref[...] = rims[start : start + count].astype(BF16)


def kernel_own(
    sizes, pieces, margin_hbm, tok_hbm, w_hbm, q_ref, kv_ref, kvt_ref, nt_ref, bias_ref, place_ref, margin_ref, tok_ref, w_ref, sems
):
    feat = w_hbm.shape[0]
    copies = [pltpu.make_async_copy(tok_hbm, tok_ref, sems.at[0])]
    for i in range(3):
        cols = pl.ds(i * feat, feat)
        copies.append(pltpu.make_async_copy(w_hbm.at[:, cols], w_ref.at[:, cols], sems.at[1 + i]))
    copies.append(pltpu.make_async_copy(margin_hbm, margin_ref, sems.at[4]))
    for copy in copies:
        copy.start()
    n_space, grid_cols, plane_rows, plane_cols = sizes
    position, member, tile_row, tile_col = own_ids(grid_cols)
    place = permutation(feat, sizes, position)
    place_ref[...] = place
    copies[0].wait()
    standard, _ = normalise(tok_ref[...])
    normed = standard.astype(BF16)
    nt_ref[:, :TOKENS] = dot_t(place, normed).astype(BF16)
    scale = 1.0 / math.sqrt(HEAD)
    copies[1].wait()
    q_ref[...] = (dot(normed, w_ref[:, :feat]).astype(BF16).astype(F32) * scale).astype(BF16)
    for i in range(2):
        copies[2 + i].wait()
        part = dot(normed, w_ref[:, (i + 1) * feat : (i + 2) * feat]).astype(BF16)
        kv_ref[:TOKENS, i * feat : (i + 1) * feat] = part
        kvt_ref[i * feat : (i + 1) * feat, :TOKENS] = part.T
    copies[4].wait()
    key = lax.broadcasted_iota(jnp.int32, (TOKENS, 128), 0)
    query = lax.broadcasted_iota(jnp.int32, (TOKENS, 128), 1)
    row = tile_row * TH + key // TW
    col = tile_col * TW + key % TW
    bias = jnp.where(live(row, col, margin_ref, plane_rows, plane_cols), 0.0, NEG)
    for i in range(0, TOKENS, 128):
        bias_ref[:TOKENS, i : i + 128] = jnp.where(key == query + i, 0.0, bias)
    padded = bias_ref.shape[0] - TOKENS
    index = lax.broadcasted_iota(jnp.int32, (padded, 128), 0)
    row = jnp.full((padded, 128), -1, jnp.int32)
    col = row
    for start, count, r0, c0, wide, *_ in pieces:
        at = index - start
        down = (at * 171) >> 9 if wide == 3 else at // wide
        here = (at >= 0) & (at < count)
        row = jnp.where(here, tile_row * TH + r0 + down, row)
        col = jnp.where(here, tile_col * TW + c0 + at - down * wide, col)
    is_open = live(row, col, margin_ref, plane_rows, plane_cols)
    is_open = is_open & (row >= 0) & (row < plane_rows) & (col >= 0) & (col < plane_cols)
    bias = jnp.where(is_open, 0.0, NEG)
    for i in range(0, TOKENS, 128):
        bias_ref[TOKENS:, i : i + 128] = bias


def kernel_attend(sizes, n_sample, spans, q_ref, cot_ref, w_ref, bias_ref, place_ref, *refs):
    n_space, grid_cols, plane_rows, plane_cols = sizes
    count = len(spans)
    toks, refs = refs[:count], refs[count + 3 :]
    kv_ref, kvt_ref, nt_ref, pb_ref, grad_ref, keep_ref, send_ref = refs[:7]
    rim_refs, refs = refs[7 : 7 + count], refs[7 + count :]
    s_s, g_s, ds_s, cm_s, qm_s, dqt_s = refs
    position, member, _, _ = own_ids(grid_cols)
    feat = w_ref.shape[0]
    keys = kv_ref.shape[0]
    padded = keys - TOKENS
    scale = 1.0 / math.sqrt(HEAD)

    parts = [r[...].astype(F32) for r in toks]
    even = (position & 1) == 0
    if paired(sizes):
        parts = [jnp.where(even, parts[1], parts[0]), jnp.where(even, parts[0], parts[1])]
    if spans[-1][1] < padded:
        parts.append(jnp.zeros((padded - spans[-1][1], feat), F32))
    standard, _ = normalise(jnp.concatenate(parts, axis=0))
    normed = standard.astype(BF16)
    for i in range(2):
        part = dot(normed, w_ref[:, (i + 1) * feat : (i + 2) * feat]).astype(BF16)
        kv_ref[TOKENS:, i * feat : (i + 1) * feat] = part
        kvt_ref[i * feat : (i + 1) * feat, TOKENS:] = part.T
    nt_ref[:, TOKENS:] = dot_t(place_ref[...], normed).astype(BF16)
    lane = lax.broadcasted_iota(jnp.int32, (TOKENS, 2 * HEAD), 1)

    def scores(head):
        slot, base = head % 2, head // 2 * 2 * HEAD
        cols = slice(base, base + 2 * HEAD)
        vcols = slice(feat + base, feat + base + 2 * HEAD)
        mine = (lane >= HEAD) if slot else (lane < HEAD)
        out = slice((head % 4) * TOKENS, (head % 4 + 1) * TOKENS)
        q, cot = q_ref[:, cols], cot_ref[:, cols]
        qm_s[out, :] = jnp.where(mine, q, jnp.zeros_like(q))
        cm_s[out, :] = jnp.where(mine, cot, jnp.zeros_like(cot))
        s_s[slot] = dot_t(kv_ref[:, cols], qm_s[out, :])
        g_s[slot] = dot_t(kv_ref[:, vcols], cm_s[out, :])

    def softmax(head):
        slot = head % 2
        out = slice(slot * TOKENS, (slot + 1) * TOKENS)
        top = jnp.full((8, TOKENS), NEG, F32)
        for r in range(0, keys, ROWS):
            x = s_s[slot, r : r + ROWS, :] + bias_ref[r : r + ROWS, :]
            top = jnp.maximum(top, jnp.max(x.reshape(ROWS // 8, 8, TOKENS), axis=0))
        top = jnp.max(top, axis=0, keepdims=True)
        total = jnp.zeros((8, TOKENS), F32)
        delta = jnp.zeros((8, TOKENS), F32)
        for r in range(0, keys, ROWS):
            x = s_s[slot, r : r + ROWS, :] + bias_ref[r : r + ROWS, :]
            e = jnp.exp(x - top)
            s_s[slot, r : r + ROWS, :] = e
            total = total + jnp.sum(e.reshape(ROWS // 8, 8, TOKENS), axis=0)
            eg = e * g_s[slot, r : r + ROWS, :]
            delta = delta + jnp.sum(eg.reshape(ROWS // 8, 8, TOKENS), axis=0)
        inv = 1.0 / jnp.sum(total, axis=0, keepdims=True)
        delta = jnp.sum(delta, axis=0, keepdims=True) * inv
        for r in range(0, keys, ROWS):
            p = s_s[slot, r : r + ROWS, :] * inv
            pb_ref[head // 2, r : r + ROWS, out] = p.astype(BF16)
            ds_s[r : r + ROWS, out] = (p * (g_s[slot, r : r + ROWS, :] - delta)).astype(BF16)

    def products(head):
        row = head * HEAD
        out = slice((head % 2) * TOKENS, (head % 2 + 1) * TOKENS)
        dqt_s[row : row + HEAD, :] = scale * dot(kvt_ref[row : row + HEAD, :], ds_s[:, out])
        if head % 2:
            base = head // 2 * 2 * HEAD
            both = slice((head % 4 - 1) * TOKENS, (head % 4 + 1) * TOKENS)
            grad_ref[:, feat + base : feat + base + 2 * HEAD] = dot(ds_s[...], qm_s[both, :]).astype(BF16)
            grad_ref[:, 2 * feat + base : 2 * feat + base + 2 * HEAD] = dot(
                pb_ref[head // 2], cm_s[both, :]
            ).astype(BF16)

    scores(0)
    for head in range(HEADS):
        if head + 1 < HEADS:
            scores(head + 1)
        softmax(head)
        products(head)
    grad_ref[:TOKENS, :feat] = dqt_s[...].T.astype(BF16)
    grad_ref[TOKENS:, :feat] = jnp.zeros((padded, feat), BF16)

    block = 3 * feat // n_sample
    for j in range(n_sample // 2):
        for target, other in ((keep_ref, 2 * j), (send_ref, 2 * j + 1)):
            cols = pl.ds(pl.multiple_of((member ^ other) * block, 128), block)
            value = dot(nt_ref[...], grad_ref[:, cols])
            target[:, j * block : (j + 1) * block] = value.astype(target.dtype)
    rim = dot_t(grad_ref[TOKENS:, feat:], w_ref[:, feat:])
    if paired(sizes):
        rows = rim_refs[0].shape[0]
        left, right = (rim[lo:hi, :] for lo, hi in spans)
        for ref, value in zip(rim_refs, (jnp.where(even, right, left), jnp.where(even, left, right))):
            wide = feat // 2
            value = jnp.concatenate([value[:, :wide], value[:, wide:]], axis=0).astype(BF16)
            for i in range(3):
                ref[:, i * wide : (i + 1) * wide] = value[i * rows : (i + 1) * rows]
    else:
        for (lo, hi), ref in zip(spans, rim_refs):
            ref[...] = rim[lo:hi, :].astype(BF16)


def kernel_mix(kvt_ref, pb_ref, att_ref, att_s):
    feat = att_ref.shape[1]
    for head in range(HEADS):
        row = head * HEAD
        out = slice((head % 2) * TOKENS, (head % 2 + 1) * TOKENS)
        att_s[row : row + HEAD, :] = dot(kvt_ref[feat + row : feat + row + HEAD, :], pb_ref[head // 2, :, out])
    att_ref[...] = att_s[...].T.astype(BF16)


def kernel_final(sizes, count, tok_ref, w_ref, index_ref, grad_ref, *refs):
    arrived, out_ref = refs[:count], refs[count]
    feat = w_ref.shape[0]
    total = dot_t(grad_ref[:TOKENS, :], w_ref[...])
    padded = index_ref.shape[1]
    parts = [r[...].astype(F32) for r in arrived]
    if paired(sizes):
        even = (lax.axis_index("space") & 1) == 0
        wide = feat // 2
        parts = [jnp.concatenate([p[:, i * wide : (i + 1) * wide] for i in range(3)], axis=0) for p in parts]
        parts = [jnp.concatenate([p[: p.shape[0] // 2], p[p.shape[0] // 2 :]], axis=1) for p in parts]
        parts = [jnp.where(even, parts[1], parts[0]), jnp.where(even, parts[0], parts[1])]
    have = sum(p.shape[0] for p in parts)
    if have < padded:
        parts.append(jnp.zeros((padded - have, feat), F32))
    rim = jnp.concatenate(parts, axis=0).astype(BF16)
    token = lax.broadcasted_iota(jnp.int32, (TOKENS, padded), 0)
    place = jnp.where(token == index_ref[...], 1.0, 0.0).astype(BF16)
    total = total + dot(place, rim)
    standard, inv = normalise(tok_ref[...])
    mean = jnp.mean(total, axis=-1, keepdims=True)
    cross = jnp.mean(total * standard, axis=-1, keepdims=True)
    out_ref[...] = ((total - mean - standard * cross) * inv).astype(BF16)


def shift(value, axis, steps):
    count = lax.axis_size(axis)
    first, last = max(0, -steps), min(count, count - steps)
    return lax.ppermute(value, axis, [(i, i + steps) for i in range(first, last)])


def span(step, length):
    if step < 0:
        return (length - HALO, length)
    if step > 0:
        return (0, HALO)
    return (0, length)


def window_span(step, length):
    if step < 0:
        return (-HALO, 0)
    if step > 0:
        return (length, length + HALO)
    return (0, length)


def struct(shape, dtype):
    return jax.ShapeDtypeStruct(shape, dtype)


def pinned(value):
    return pltpu.with_memory_space_constraint(value, pltpu.HBM)


def cost(flops, nbytes, exps=0):
    return pl.CostEstimate(flops=int(flops), bytes_accessed=int(nbytes), transcendentals=int(exps))


def exchange(value, axis, mask):
    count = lax.axis_size(axis)
    return lax.ppermute(value, axis, [(i, i ^ mask) for i in range(count)])


def local(tokens, cotangent, weight, margins):
    feat = weight.shape[0]
    tok, cot = tokens[0, 0], cotangent[0, 0]
    n_space, n_sample = lax.axis_size("space"), lax.axis_size("sample")
    grid_cols = min(8, n_space)
    grid_rows = n_space // grid_cols
    sizes = (n_space, grid_cols, grid_rows * TH, grid_cols * TW)
    masks = row_masks(sizes)
    row_steps = (-1, 0, 1) if grid_rows > 1 else (0,)
    steps = [(r, c) for r in row_steps for c in (-1, 0, 1) if (r, c) != (0, 0)]
    counts, pieces, sources = [], [], []
    way = -1 if paired(sizes) else 1
    for r, c in steps:
        (r0, r1), (c0, c1) = window_span(r, TH), window_span(c, TW)
        pieces.append((sum(counts), (r1 - r0) * (c1 - c0), r0, c0, c1 - c0, span(r, TH)[0], span(c, TW)[0]))
        rr, cc = np.meshgrid(np.arange(*span(way * r, TH)), np.arange(*span(way * c, TW)), indexing="ij")
        sources.append((rr * TW + cc).ravel())
        counts.append(pieces[-1][1])
    halo = sum(counts)
    padded = -(-halo // 128) * 128
    keys = TOKENS + padded
    rim_index = np.concatenate([*sources, np.full(padded - halo, -1)]).astype(np.int32)[None, :]
    ends = np.cumsum([0, *counts])
    spans = [(int(a), int(b)) for a, b in zip(ends[:-1], ends[1:])]

    rims = pl.pallas_call(
        functools.partial(kernel_pack, sizes, pieces),
        out_shape=[struct((n, feat), BF16) for n in counts],
        in_specs=[hbm()],
        out_specs=[vmem()] * len(counts),
        scratch_shapes=[pltpu.VMEM(tok.shape, BF16), pltpu.SemaphoreType.DMA],
        compiler_params=params(16),
        cost_estimate=cost(2 * halo * TOKENS * feat, PACK),
        name="pack",
    )(pinned(tok))
    if paired(sizes):
        halo_tokens = [exchange(v, "space", m) for v, m in zip(rims, masks)]
        halo_tokens += [jnp.zeros_like(rims[0])] * (2 - len(masks))
    else:
        halo_tokens = [shift(v, "space", -(r * grid_cols + c)) for v, (r, c) in zip(rims, steps)]

    q, kv, kvt, nt, bias, place = pl.pallas_call(
        functools.partial(kernel_own, sizes, pieces),
        out_shape=(
            struct((TOKENS, feat), BF16),
            struct((keys, 2 * feat), BF16),
            struct((2 * feat, keys), BF16),
            struct((feat, keys), BF16),
            struct((keys, TOKENS), F32),
            struct((feat, feat), BF16),
        ),
        in_specs=[hbm()] * 3,
        out_specs=[vmem()] * 6,
        scratch_shapes=[
            pltpu.SMEM(margins.shape, jnp.int32),
            pltpu.VMEM(tok.shape, BF16),
            pltpu.VMEM(weight.shape, BF16),
            pltpu.SemaphoreType.DMA((5,)),
        ],
        compiler_params=params(OWN),
        cost_estimate=cost(8 * TOKENS * feat * feat, 7e6),
        name="own",
    )(*(pinned(a) for a in (margins, tok, weight)))

    rim_shape = (2 * counts[0] // 3, 3 * feat // 2)
    outs = pl.pallas_call(
        functools.partial(kernel_attend, sizes, n_sample, spans),
        out_shape=(
            *[struct(a.shape, a.dtype) for a in (kv, kvt, nt)],
            struct((HEADS // 2, keys, 2 * TOKENS), BF16),
            struct((keys, 3 * feat), BF16),
            struct((feat, 3 * feat // 2), F32),
            struct((feat, 3 * feat // 2), BF16),
            *[struct(rim_shape if paired(sizes) else (n, feat), BF16) for n in counts],
        ),
        in_specs=[vmem()] * (5 + len(counts) + 3),
        out_specs=[vmem()] * (7 + len(counts)),
        input_output_aliases={5 + len(counts) + i: i for i in range(3)},
        scratch_shapes=[
            pltpu.VMEM((2, keys, TOKENS), F32),
            pltpu.VMEM((2, keys, TOKENS), F32),
            pltpu.VMEM((keys, 2 * TOKENS), BF16),
            pltpu.VMEM((4 * TOKENS, 2 * HEAD), BF16),
            pltpu.VMEM((4 * TOKENS, 2 * HEAD), BF16),
            pltpu.VMEM((feat, TOKENS), F32),
        ],
        compiler_params=params(),
        cost_estimate=cost(48 * TOKENS * keys * feat, 6e6, TOKENS * keys * HEADS),
        name="attend",
    )(q, cot, weight, bias, place, *halo_tokens, kv, kvt, nt)
    kvt, prob = outs[1], outs[3]
    grads, keep, send = outs[4:7]
    rims = list(outs[7:])

    total = keep + exchange(send, "sample", 1).astype(F32)
    half = row_split(feat, n_space) * n_space
    first, second = total[:half], total[half:]
    col_masks = [1 << bit for bit in range((n_sample - 1).bit_length() - 1, 0, -1)]
    arrived = []
    if not paired(sizes):
        arrived = [shift(rim, "space", r * grid_cols + c) for (r, c), rim in zip(steps, rims)]

    def by_cols(value):
        for mask in col_masks:
            n = value.shape[1] // 2
            got = exchange(value[:, n:].astype(BF16), "sample", mask)
            value = value[:, :n] + got.astype(F32)
        return value

    def by_rows(value, riders):
        for i, mask in enumerate(masks):
            n = value.shape[0] // 2
            out = value[n:].astype(BF16)
            if riders:
                out = jnp.concatenate([out, riders[i]], axis=0)
            got = exchange(out, "space", mask)
            if riders:
                arrived.append(got[n:])
            value = value[:n] + got[:n].astype(F32)
        return value

    upper = by_rows(by_cols(first), [])
    lower = by_cols(by_rows(second, rims if paired(sizes) else []))
    weight_grad = jnp.concatenate([upper, lower], axis=0)

    attention = pl.pallas_call(
        kernel_mix,
        out_shape=struct((TOKENS, feat), BF16),
        in_specs=[vmem()] * 2,
        out_specs=vmem(),
        scratch_shapes=[pltpu.VMEM((feat, TOKENS), F32)],
        compiler_params=params(8),
        cost_estimate=cost(8 * TOKENS * keys * feat, 6e6),
        name="mix",
    )(kvt, prob)
    arrived += [jnp.zeros_like(rim) for rim in rims[len(arrived) :]]

    token_grad = pl.pallas_call(
        functools.partial(kernel_final, sizes, len(steps)),
        out_shape=struct((TOKENS, feat), BF16),
        in_specs=[vmem()] * (4 + len(steps)),
        out_specs=vmem(),
        compiler_params=params(16),
        cost_estimate=cost(6 * TOKENS * feat * feat, 5e6),
        name="final",
    )(tok, weight, jnp.asarray(rim_index), grads, *arrived)
    return (attention[None, None], token_grad[None, None], weight_grad)


def solution(mesh):
    return jax.shard_map(
        local,
        mesh=mesh,
        in_specs=(
            P(("groups", "sample"), "space", None, None),
            P(("groups", "sample"), "space", None, None),
            P("groups", None),
            P(("groups", "sample"), None),
        ),
        out_specs=(
            P(("groups", "sample"), "space", None, None),
            P(("groups", "sample"), "space", None, None),
            P(("groups", "space"), "sample"),
        ),
        check_vma=False,
    )
```

```python
import functools
import math

import jax
import jax.numpy as jnp
import numpy as np
from jax import lax
from jax.experimental import pallas as pl
from jax.experimental.pallas import tpu as pltpu
from jax.sharding import PartitionSpec as P

HEADS = 8
HEAD = 64
TH = 16
TW = 32
HALO = 3
TOKENS = TH * TW
NEG = -1e30
TIES = (0,)
LAST = (((1,), (1,)), ((), ()))
F32 = jnp.float32
BF16 = jnp.bfloat16
ROWS = 64

vmem = functools.partial(pl.BlockSpec, memory_space=pltpu.VMEM)
anywhere = functools.partial(pl.BlockSpec, memory_space=pl.ANY)
hbm = functools.partial(pl.BlockSpec, memory_space=pltpu.HBM)


def params(mib=24):
    return pltpu.CompilerParams(vmem_limit_bytes=mib * 1024 * 1024)


def dot(a, b):
    return jnp.dot(a, b, preferred_element_type=F32)


def dot_t(a, b):
    return lax.dot_general(a, b, LAST, preferred_element_type=F32)


def normalise(tok):
    tok = tok.astype(F32)
    centred = tok - jnp.mean(tok, axis=-1, keepdims=True)
    inv = lax.rsqrt(jnp.mean(centred * centred, axis=-1, keepdims=True) + 1e-05)
    return centred * inv, inv


def own_ids(cols):
    position = lax.axis_index("space")
    member = lax.axis_index("sample")
    return position, member, position // cols, position % cols


def live(row, col, margin_ref, rows, cols):
    return (
        (row >= margin_ref[0, 0])
        & (row < rows - margin_ref[0, 1])
        & (col >= margin_ref[0, 2])
        & (col < cols - margin_ref[0, 3])
    )


def row_masks(sizes):
    bits = (sizes[0] - 1).bit_length()
    one_row = sizes[1] == sizes[0]
    return [((2 << i) - 1) if one_row else (1 << i) for i in range(bits)]


def paired(sizes):
    return sizes[1] == sizes[0] and sizes[0] in (2, 4)


def row_split(feat, n_space):
    size = feat // n_space
    return size // 2 // 16 * 16 if size >= 64 else size // 2


def permutation(feat, sizes, position):
    masks = row_masks(sizes)
    size = feat // sizes[0]
    upper = row_split(feat, sizes[0])
    row = lax.broadcasted_iota(jnp.int32, (feat, 128), 0)
    below = row >= upper * sizes[0]
    at = jnp.where(below, row - upper * sizes[0], row)
    relative = jnp.where(below, at // (size - upper), at // upper)
    rest = at - relative * jnp.where(below, size - upper, upper)
    space = jnp.zeros_like(row) + position
    for i, mask in enumerate(masks):
        space = space ^ (((relative >> (len(masks) - 1 - i)) & 1) * mask)
    source = space * size + jnp.where(below, upper, 0) + rest
    col = lax.broadcasted_iota(jnp.int32, (feat, 128), 1)
    return jnp.concatenate(
        [jnp.where(col + i == source, 1.0, 0.0).astype(BF16) for i in range(0, feat, 128)], axis=1
    )


def kernel_pack(sizes, pieces, tok_hbm, *refs):
    rim_refs, (tok_ref, sem) = refs[: len(pieces)], refs[len(pieces) :]
    copy = pltpu.make_async_copy(tok_hbm, tok_ref, sem)
    copy.start()
    even = (lax.axis_index("space") & 1) == 0
    total = sum(p[1] for p in pieces)
    rows = -(-total // 16) * 16
    index = lax.broadcasted_iota(jnp.int32, (rows, TOKENS), 0)
    token = lax.broadcasted_iota(jnp.int32, (rows, TOKENS), 1)
    wanted = jnp.full((rows, TOKENS), -1, jnp.int32)
    for i, (start, count, _, _, wide, r0, c0) in enumerate(pieces):
        at = index - start
        down = (at * 171) >> 9 if wide == 3 else at // wide
        source = (r0 + down) * TW + c0 + at - down * wide
        if paired(sizes):
            source = source + jnp.where(even, 0, pieces[1 - i][6] - c0)
        wanted = jnp.where((at >= 0) & (at < count), source, wanted)
    select = jnp.where(wanted == token, 1.0, 0.0).astype(BF16)
    copy.wait()
    rims = dot(select, tok_ref[...])
    for (start, count, *_), ref in zip(pieces, rim_refs):
        ref[...] = rims[start : start + count].astype(BF16)


def kernel_own(
    sizes, pieces, margin_hbm, tok_ref, w_hbm, q_ref, kv_ref, kvt_ref, nt_ref, bias_ref, place_ref, margin_ref, w_ref, sems
):
    feat = w_hbm.shape[0]
    copies = []
    for i in range(3):
        cols = pl.ds(i * feat, feat)
        copies.append(pltpu.make_async_copy(w_hbm.at[:, cols], w_ref.at[:, cols], sems.at[i]))
    copies.append(pltpu.make_async_copy(margin_hbm, margin_ref, sems.at[3]))
    for copy in copies:
        copy.start()
    n_space, grid_cols, plane_rows, plane_cols = sizes
    position, member, tile_row, tile_col = own_ids(grid_cols)
    place = permutation(feat, sizes, position)
    place_ref[...] = place
    standard, _ = normalise(tok_ref[...])
    normed = standard.astype(BF16)
    nt_ref[:, :TOKENS] = dot_t(place, normed).astype(BF16)
    scale = 1.0 / math.sqrt(HEAD)
    copies[0].wait()
    q_ref[...] = (dot(normed, w_ref[:, :feat]).astype(BF16).astype(F32) * scale).astype(BF16)
    for i in range(2):
        copies[1 + i].wait()
        part = dot(normed, w_ref[:, (i + 1) * feat : (i + 2) * feat]).astype(BF16)
        kv_ref[:TOKENS, i * feat : (i + 1) * feat] = part
        kvt_ref[i * feat : (i + 1) * feat, :TOKENS] = part.T
    copies[3].wait()
    key = lax.broadcasted_iota(jnp.int32, (TOKENS, 128), 0)
    query = lax.broadcasted_iota(jnp.int32, (TOKENS, 128), 1)
    row = tile_row * TH + key // TW
    col = tile_col * TW + key % TW
    bias = jnp.where(live(row, col, margin_ref, plane_rows, plane_cols), 0.0, NEG)
    for i in range(0, TOKENS, 128):
        bias_ref[:TOKENS, i : i + 128] = jnp.where(key == query + i, 0.0, bias)
    padded = bias_ref.shape[0] - TOKENS
    index = lax.broadcasted_iota(jnp.int32, (padded, 128), 0)
    row = jnp.full((padded, 128), -1, jnp.int32)
    col = row
    for start, count, r0, c0, wide, *_ in pieces:
        at = index - start
        down = (at * 171) >> 9 if wide == 3 else at // wide
        here = (at >= 0) & (at < count)
        row = jnp.where(here, tile_row * TH + r0 + down, row)
        col = jnp.where(here, tile_col * TW + c0 + at - down * wide, col)
    is_open = live(row, col, margin_ref, plane_rows, plane_cols)
    is_open = is_open & (row >= 0) & (row < plane_rows) & (col >= 0) & (col < plane_cols)
    bias = jnp.where(is_open, 0.0, NEG)
    for i in range(0, TOKENS, 128):
        bias_ref[TOKENS:, i : i + 128] = bias


def kernel_attend(sizes, n_sample, spans, q_ref, cot_ref, w_ref, bias_ref, place_ref, *refs):
    n_space, grid_cols, plane_rows, plane_cols = sizes
    count = len(spans)
    toks, refs = refs[:count], refs[count + 3 :]
    kv_ref, kvt_ref, nt_ref, pb_ref, grad_ref, keep_ref, send_ref, *refs = refs
    s_s, g_s, ds_s, cm_s, qm_s, dqt_s = refs
    position, member, _, _ = own_ids(grid_cols)
    feat = w_ref.shape[0]
    keys = kv_ref.shape[0]
    padded = keys - TOKENS
    scale = 1.0 / math.sqrt(HEAD)

    parts = [r[...].astype(F32) for r in toks]
    even = (position & 1) == 0
    if paired(sizes):
        parts = [jnp.where(even, parts[1], parts[0]), jnp.where(even, parts[0], parts[1])]
    if spans[-1][1] < padded:
        parts.append(jnp.zeros((padded - spans[-1][1], feat), F32))
    standard, _ = normalise(jnp.concatenate(parts, axis=0))
    normed = standard.astype(BF16)
    for i in range(2):
        part = dot(normed, w_ref[:, (i + 1) * feat : (i + 2) * feat]).astype(BF16)
        kv_ref[TOKENS:, i * feat : (i + 1) * feat] = part
        kvt_ref[i * feat : (i + 1) * feat, TOKENS:] = part.T
    nt_ref[:, TOKENS:] = dot_t(place_ref[...], normed).astype(BF16)
    lane = lax.broadcasted_iota(jnp.int32, (TOKENS, 2 * HEAD), 1)

    def scores(head):
        slot, base = head % 2, head // 2 * 2 * HEAD
        cols = slice(base, base + 2 * HEAD)
        vcols = slice(feat + base, feat + base + 2 * HEAD)
        mine = (lane >= HEAD) if slot else (lane < HEAD)
        out = slice((head % 4) * TOKENS, (head % 4 + 1) * TOKENS)
        q, cot = q_ref[:, cols], cot_ref[:, cols]
        qm_s[out, :] = jnp.where(mine, q, jnp.zeros_like(q))
        cm_s[out, :] = jnp.where(mine, cot, jnp.zeros_like(cot))
        s_s[slot] = dot_t(kv_ref[:, cols], qm_s[out, :])
        g_s[slot] = dot_t(kv_ref[:, vcols], cm_s[out, :])

    def softmax(head):
        slot = head % 2
        out = slice(slot * TOKENS, (slot + 1) * TOKENS)
        top = jnp.full((8, TOKENS), NEG, F32)
        for r in range(0, keys, ROWS):
            x = s_s[slot, r : r + ROWS, :] + bias_ref[r : r + ROWS, :]
            top = jnp.maximum(top, jnp.max(x.reshape(ROWS // 8, 8, TOKENS), axis=0))
        top = jnp.max(top, axis=0, keepdims=True)
        total = jnp.zeros((8, TOKENS), F32)
        delta = jnp.zeros((8, TOKENS), F32)
        for r in range(0, keys, ROWS):
            x = s_s[slot, r : r + ROWS, :] + bias_ref[r : r + ROWS, :]
            e = jnp.exp(x - top)
            s_s[slot, r : r + ROWS, :] = e
            total = total + jnp.sum(e.reshape(ROWS // 8, 8, TOKENS), axis=0)
            eg = e * g_s[slot, r : r + ROWS, :]
            delta = delta + jnp.sum(eg.reshape(ROWS // 8, 8, TOKENS), axis=0)
        inv = 1.0 / jnp.sum(total, axis=0, keepdims=True)
        delta = jnp.sum(delta, axis=0, keepdims=True) * inv
        for r in range(0, keys, ROWS):
            p = s_s[slot, r : r + ROWS, :] * inv
            pb_ref[head // 2, r : r + ROWS, out] = p.astype(BF16)
            ds_s[r : r + ROWS, out] = (p * (g_s[slot, r : r + ROWS, :] - delta)).astype(BF16)

    def products(head):
        row = head * HEAD
        out = slice((head % 2) * TOKENS, (head % 2 + 1) * TOKENS)
        dqt_s[row : row + HEAD, :] = scale * dot(kvt_ref[row : row + HEAD, :], ds_s[:, out])
        if head % 2:
            base = head // 2 * 2 * HEAD
            both = slice((head % 4 - 1) * TOKENS, (head % 4 + 1) * TOKENS)
            grad_ref[:, feat + base : feat + base + 2 * HEAD] = dot(ds_s[...], qm_s[both, :]).astype(BF16)
            grad_ref[:, 2 * feat + base : 2 * feat + base + 2 * HEAD] = dot(
                pb_ref[head // 2], cm_s[both, :]
            ).astype(BF16)

    scores(0)
    for head in range(HEADS):
        if head + 1 < HEADS:
            scores(head + 1)
        softmax(head)
        products(head)
    grad_ref[:TOKENS, :feat] = dqt_s[...].T.astype(BF16)
    grad_ref[TOKENS:, :feat] = jnp.zeros((padded, feat), BF16)

    block = 3 * feat // n_sample
    for j in range(n_sample // 2):
        for target, other in ((keep_ref, 2 * j), (send_ref, 2 * j + 1)):
            cols = pl.ds(pl.multiple_of((member ^ other) * block, 128), block)
            value = dot(nt_ref[...], grad_ref[:, cols])
            target[:, j * block : (j + 1) * block] = value.astype(target.dtype)


def kernel_mix(sizes, spans, kvt_ref, pb_ref, grad_ref, w_ref, att_ref, *refs):
    rim_refs, att_s = refs[:-1], refs[-1]
    feat = att_ref.shape[1]
    even = (lax.axis_index("space") & 1) == 0
    rim = dot_t(grad_ref[TOKENS:, feat:], w_ref[:, feat:])
    if paired(sizes):
        rows = rim_refs[0].shape[0]
        left, right = (rim[lo:hi, :] for lo, hi in spans)
        for ref, value in zip(rim_refs, (jnp.where(even, right, left), jnp.where(even, left, right))):
            wide = feat // 2
            value = jnp.concatenate([value[:, :wide], value[:, wide:]], axis=0).astype(BF16)
            for i in range(3):
                ref[:, i * wide : (i + 1) * wide] = value[i * rows : (i + 1) * rows]
    else:
        for (lo, hi), ref in zip(spans, rim_refs):
            ref[...] = rim[lo:hi, :].astype(BF16)
    for head in range(HEADS):
        row = head * HEAD
        out = slice((head % 2) * TOKENS, (head % 2 + 1) * TOKENS)
        att_s[row : row + HEAD, :] = dot(kvt_ref[feat + row : feat + row + HEAD, :], pb_ref[head // 2, :, out])
    att_ref[...] = att_s[...].T.astype(BF16)


def kernel_final(sizes, count, tok_ref, w_ref, index_ref, grad_ref, *refs):
    arrived, out_ref = refs[:count], refs[-1]
    feat = w_ref.shape[0]
    total = dot_t(grad_ref[:TOKENS, :], w_ref[...])
    padded = index_ref.shape[1]
    parts = [r[...].astype(F32) for r in arrived]
    if paired(sizes):
        even = (lax.axis_index("space") & 1) == 0
        wide = feat // 2
        parts = [jnp.concatenate([p[:, i * wide : (i + 1) * wide] for i in range(3)], axis=0) for p in parts]
        parts = [jnp.concatenate([p[: p.shape[0] // 2], p[p.shape[0] // 2 :]], axis=1) for p in parts]
        parts = [jnp.where(even, parts[1], parts[0]), jnp.where(even, parts[0], parts[1])]
    have = sum(p.shape[0] for p in parts)
    if have < padded:
        parts.append(jnp.zeros((padded - have, feat), F32))
    rim = jnp.concatenate(parts, axis=0).astype(BF16)
    token = lax.broadcasted_iota(jnp.int32, (TOKENS, padded), 0)
    place = jnp.where(token == index_ref[...], 1.0, 0.0).astype(BF16)
    total = total + dot(place, rim)
    standard, inv = normalise(tok_ref[...])
    mean = jnp.mean(total, axis=-1, keepdims=True)
    cross = jnp.mean(total * standard, axis=-1, keepdims=True)
    out_ref[...] = ((total - mean - standard * cross) * inv).astype(BF16)


def shift(value, axis, steps):
    count = lax.axis_size(axis)
    first, last = max(0, -steps), min(count, count - steps)
    return lax.ppermute(value, axis, [(i, i + steps) for i in range(first, last)])


def span(step, length):
    if step < 0:
        return (length - HALO, length)
    if step > 0:
        return (0, HALO)
    return (0, length)


def window_span(step, length):
    if step < 0:
        return (-HALO, 0)
    if step > 0:
        return (length, length + HALO)
    return (0, length)


def struct(shape, dtype):
    return jax.ShapeDtypeStruct(shape, dtype)


def pinned(value):
    return pltpu.with_memory_space_constraint(value, pltpu.HBM)


def cost(flops, nbytes, exps=0):
    return pl.CostEstimate(flops=int(flops), bytes_accessed=int(nbytes), transcendentals=int(exps))


def exchange(value, axis, mask):
    count = lax.axis_size(axis)
    return lax.ppermute(value, axis, [(i, i ^ mask) for i in range(count)])


def local(tokens, cotangent, weight, margins):
    feat = weight.shape[0]
    tok, cot = tokens[0, 0], cotangent[0, 0]
    n_space, n_sample = lax.axis_size("space"), lax.axis_size("sample")
    grid_cols = min(8, n_space)
    grid_rows = n_space // grid_cols
    sizes = (n_space, grid_cols, grid_rows * TH, grid_cols * TW)
    masks = row_masks(sizes)
    row_steps = (-1, 0, 1) if grid_rows > 1 else (0,)
    steps = [(r, c) for r in row_steps for c in (-1, 0, 1) if (r, c) != (0, 0)]
    counts, pieces, sources = [], [], []
    way = -1 if paired(sizes) else 1
    for r, c in steps:
        (r0, r1), (c0, c1) = window_span(r, TH), window_span(c, TW)
        pieces.append((sum(counts), (r1 - r0) * (c1 - c0), r0, c0, c1 - c0, span(r, TH)[0], span(c, TW)[0]))
        rr, cc = np.meshgrid(np.arange(*span(way * r, TH)), np.arange(*span(way * c, TW)), indexing="ij")
        sources.append((rr * TW + cc).ravel())
        counts.append(pieces[-1][1])
    halo = sum(counts)
    padded = -(-halo // 128) * 128
    keys = TOKENS + padded
    rim_index = np.concatenate([*sources, np.full(padded - halo, -1)]).astype(np.int32)[None, :]
    ends = np.cumsum([0, *counts])
    spans = [(int(a), int(b)) for a, b in zip(ends[:-1], ends[1:])]

    *rims, tok_near = pl.pallas_call(
        functools.partial(kernel_pack, sizes, pieces),
        out_shape=[*[struct((n, feat), BF16) for n in counts], struct(tok.shape, BF16)],
        in_specs=[hbm()],
        out_specs=[vmem()] * (len(counts) + 1),
        scratch_shapes=[pltpu.SemaphoreType.DMA],
        compiler_params=params(16),
        cost_estimate=cost(2 * halo * TOKENS * feat, 1e6),
        name="pack",
    )(pinned(tok))
    if paired(sizes):
        halo_tokens = [exchange(v, "space", m) for v, m in zip(rims, masks)]
        halo_tokens += [jnp.zeros_like(rims[0])] * (2 - len(masks))
    else:
        halo_tokens = [shift(v, "space", -(r * grid_cols + c)) for v, (r, c) in zip(rims, steps)]

    q, kv, kvt, nt, bias, place = pl.pallas_call(
        functools.partial(kernel_own, sizes, pieces),
        out_shape=(
            struct((TOKENS, feat), BF16),
            struct((keys, 2 * feat), BF16),
            struct((2 * feat, keys), BF16),
            struct((feat, keys), BF16),
            struct((keys, TOKENS), F32),
            struct((feat, feat), BF16),
        ),
        in_specs=[hbm(), vmem(), hbm()],
        out_specs=[vmem()] * 6,
        scratch_shapes=[
            pltpu.SMEM(margins.shape, jnp.int32),
            pltpu.VMEM(weight.shape, BF16),
            pltpu.SemaphoreType.DMA((4,)),
        ],
        compiler_params=params(),
        cost_estimate=cost(8 * TOKENS * feat * feat, 7e6),
        name="own",
    )(pinned(margins), tok_near, pinned(weight))

    rim_shape = (2 * counts[0] // 3, 3 * feat // 2)
    outs = pl.pallas_call(
        functools.partial(kernel_attend, sizes, n_sample, spans),
        out_shape=(
            *[struct(a.shape, a.dtype) for a in (kv, kvt, nt)],
            struct((HEADS // 2, keys, 2 * TOKENS), BF16),
            struct((keys, 3 * feat), BF16),
            struct((feat, 3 * feat // 2), F32),
            struct((feat, 3 * feat // 2), BF16),
        ),
        in_specs=[vmem()] * (5 + len(counts) + 3),
        out_specs=[vmem()] * 7,
        input_output_aliases={5 + len(counts) + i: i for i in range(3)},
        scratch_shapes=[
            pltpu.VMEM((2, keys, TOKENS), F32),
            pltpu.VMEM((2, keys, TOKENS), F32),
            pltpu.VMEM((keys, 2 * TOKENS), BF16),
            pltpu.VMEM((4 * TOKENS, 2 * HEAD), BF16),
            pltpu.VMEM((4 * TOKENS, 2 * HEAD), BF16),
            pltpu.VMEM((feat, TOKENS), F32),
        ],
        compiler_params=params(),
        cost_estimate=cost(48 * TOKENS * keys * feat, 6e6, TOKENS * keys * HEADS),
        name="attend",
    )(q, cot, weight, bias, place, *halo_tokens, kv, kvt, nt)
    kvt, prob, grads, keep, send = outs[1], *outs[3:]

    attention, *rims = pl.pallas_call(
        functools.partial(kernel_mix, sizes, spans),
        out_shape=(
            struct((TOKENS, feat), BF16),
            *[struct(rim_shape if paired(sizes) else (n, feat), BF16) for n in counts],
        ),
        in_specs=[vmem()] * 4,
        out_specs=[vmem()] * (1 + len(counts)),
        scratch_shapes=[pltpu.VMEM((feat, TOKENS), F32)],
        compiler_params=params(12),
        cost_estimate=cost(8 * TOKENS * keys * feat, 6e6),
        name="mix",
    )(kvt, prob, grads, weight)

    total = keep + exchange(send, "sample", 1).astype(F32)
    half = row_split(feat, n_space) * n_space
    first, second = total[:half], total[half:]
    col_masks = [1 << bit for bit in range((n_sample - 1).bit_length() - 1, 0, -1)]
    arrived = []
    if not paired(sizes):
        arrived = [shift(rim, "space", r * grid_cols + c) for (r, c), rim in zip(steps, rims)]

    def cut(value, axis):
        dim = 0 if axis == "space" else 1
        return jnp.split(value, 2, axis=dim)

    upper, lower = first, second
    over_rows = [("space", mask) for mask in masks]
    over_cols = [("sample", mask) for mask in col_masks]
    after, step = [], 0
    for one, two in zip(over_cols + over_rows, over_rows + over_cols):
        upper, out = cut(upper, one[0])
        got = exchange(out.astype(BF16), *one)
        lower, out = cut(lower, two[0])
        out = out.astype(BF16)
        ride = paired(sizes) and two[0] == "space"
        if ride:
            out = jnp.concatenate([out, rims[step]], axis=0)
        other = exchange(out, *two)
        if step in TIES:
            got, other = lax.optimization_barrier((got, other))
        if ride:
            arrived.append(other[lower.shape[0] :])
        if step == len(over_cols):
            after.append(got)
        upper = upper + got.astype(F32)
        lower = lower + other[: lower.shape[0]].astype(F32)
        step += 1
    weight_grad = jnp.concatenate([upper, lower], axis=0)

    token_grad = pl.pallas_call(
        functools.partial(kernel_final, sizes, len(steps)),
        out_shape=struct((TOKENS, feat), BF16),
        in_specs=[vmem()] * (4 + len(steps)) + [anywhere()] * len(after),
        out_specs=vmem(),
        compiler_params=params(16),
        cost_estimate=cost(6 * TOKENS * feat * feat, 5e6),
        name="final",
    )(tok_near, weight, jnp.asarray(rim_index), grads, *arrived, *after)
    return (attention[None, None], token_grad[None, None], weight_grad)


def solution(mesh):
    return jax.shard_map(
        local,
        mesh=mesh,
        in_specs=(
            P(("groups", "sample"), "space", None, None),
            P(("groups", "sample"), "space", None, None),
            P("groups", None),
            P(("groups", "sample"), None),
        ),
        out_specs=(
            P(("groups", "sample"), "space", None, None),
            P(("groups", "sample"), "space", None, None),
            P(("groups", "space"), "sample"),
        ),
        check_vma=False,
    )
```

```python
import functools
import math

import jax
import jax.numpy as jnp
import numpy as np
from jax import lax
from jax.experimental import pallas as pl
from jax.experimental.pallas import tpu as pltpu
from jax.sharding import PartitionSpec as P

HEADS = 8
HEAD = 64
TH = 16
TW = 32
HALO = 3
TOKENS = TH * TW
NEG = -1e30
TIES = (0,)
LAST = (((1,), (1,)), ((), ()))
F32 = jnp.float32
BF16 = jnp.bfloat16
ROWS = 64

vmem = functools.partial(pl.BlockSpec, memory_space=pltpu.VMEM)
anywhere = functools.partial(pl.BlockSpec, memory_space=pl.ANY)
hbm = functools.partial(pl.BlockSpec, memory_space=pltpu.HBM)


def params(mib=24):
    return pltpu.CompilerParams(vmem_limit_bytes=mib * 1024 * 1024)


def dot(a, b):
    return jnp.dot(a, b, preferred_element_type=F32)


def dot_t(a, b):
    return lax.dot_general(a, b, LAST, preferred_element_type=F32)


def normalise(tok):
    tok = tok.astype(F32)
    centred = tok - jnp.mean(tok, axis=-1, keepdims=True)
    inv = lax.rsqrt(jnp.mean(centred * centred, axis=-1, keepdims=True) + 1e-05)
    return centred * inv, inv


def own_ids(cols):
    position = lax.axis_index("space")
    member = lax.axis_index("sample")
    return position, member, position // cols, position % cols


def live(row, col, margin_ref, rows, cols):
    return (
        (row >= margin_ref[0, 0])
        & (row < rows - margin_ref[0, 1])
        & (col >= margin_ref[0, 2])
        & (col < cols - margin_ref[0, 3])
    )


def row_masks(sizes):
    bits = (sizes[0] - 1).bit_length()
    one_row = sizes[1] == sizes[0]
    return [((2 << i) - 1) if one_row else (1 << i) for i in range(bits)]


def paired(sizes):
    return sizes[1] == sizes[0] and sizes[0] in (2, 4)


def row_split(feat, n_space):
    size = feat // n_space
    return size // 2 // 16 * 16 if size >= 64 else size // 2


def permutation(feat, sizes, position):
    masks = row_masks(sizes)
    size = feat // sizes[0]
    upper = row_split(feat, sizes[0])
    row = lax.broadcasted_iota(jnp.int32, (feat, 128), 0)
    below = row >= upper * sizes[0]
    at = jnp.where(below, row - upper * sizes[0], row)
    relative = jnp.where(below, at // (size - upper), at // upper)
    rest = at - relative * jnp.where(below, size - upper, upper)
    space = jnp.zeros_like(row) + position
    for i, mask in enumerate(masks):
        space = space ^ (((relative >> (len(masks) - 1 - i)) & 1) * mask)
    source = space * size + jnp.where(below, upper, 0) + rest
    col = lax.broadcasted_iota(jnp.int32, (feat, 128), 1)
    return jnp.concatenate(
        [jnp.where(col + i == source, 1.0, 0.0).astype(BF16) for i in range(0, feat, 128)], axis=1
    )


def kernel_pack(sizes, pieces, tok_hbm, *refs):
    rim_refs, (tok_ref, sem) = refs[: len(pieces)], refs[len(pieces) :]
    copy = pltpu.make_async_copy(tok_hbm, tok_ref, sem)
    copy.start()
    even = (lax.axis_index("space") & 1) == 0
    total = sum(p[1] for p in pieces)
    rows = -(-total // 16) * 16
    index = lax.broadcasted_iota(jnp.int32, (rows, TOKENS), 0)
    token = lax.broadcasted_iota(jnp.int32, (rows, TOKENS), 1)
    wanted = jnp.full((rows, TOKENS), -1, jnp.int32)
    for i, (start, count, _, _, wide, r0, c0) in enumerate(pieces):
        at = index - start
        down = (at * 171) >> 9 if wide == 3 else at // wide
        source = (r0 + down) * TW + c0 + at - down * wide
        if paired(sizes):
            source = source + jnp.where(even, 0, pieces[1 - i][6] - c0)
        wanted = jnp.where((at >= 0) & (at < count), source, wanted)
    select = jnp.where(wanted == token, 1.0, 0.0).astype(BF16)
    copy.wait()
    rims = dot(select, tok_ref[...])
    for (start, count, *_), ref in zip(pieces, rim_refs):
        ref[...] = rims[start : start + count].astype(BF16)


def kernel_own(
    sizes, pieces, margin_hbm, tok_ref, w_hbm, q_ref, kv_ref, kvt_ref, nt_ref, bias_ref, place_ref, w_ref, margin_ref, sems
):
    feat = w_hbm.shape[0]
    copies = []
    for i in range(3):
        cols = pl.ds(i * feat, feat)
        copies.append(pltpu.make_async_copy(w_hbm.at[:, cols], w_ref.at[:, cols], sems.at[i]))
    copies.append(pltpu.make_async_copy(margin_hbm, margin_ref, sems.at[3]))
    for copy in copies:
        copy.start()
    n_space, grid_cols, plane_rows, plane_cols = sizes
    position, member, tile_row, tile_col = own_ids(grid_cols)
    place = permutation(feat, sizes, position)
    place_ref[...] = place
    standard, _ = normalise(tok_ref[...])
    normed = standard.astype(BF16)
    nt_ref[:, :TOKENS] = dot_t(place, normed).astype(BF16)
    scale = 1.0 / math.sqrt(HEAD)
    copies[0].wait()
    q_ref[...] = (dot(normed, w_ref[:, :feat]).astype(BF16).astype(F32) * scale).astype(BF16)
    for i in range(2):
        copies[1 + i].wait()
        part = dot(normed, w_ref[:, (i + 1) * feat : (i + 2) * feat]).astype(BF16)
        kv_ref[:TOKENS, i * feat : (i + 1) * feat] = part
        kvt_ref[i * feat : (i + 1) * feat, :TOKENS] = part.T
    copies[3].wait()
    key = lax.broadcasted_iota(jnp.int32, (TOKENS, 128), 0)
    query = lax.broadcasted_iota(jnp.int32, (TOKENS, 128), 1)
    row = tile_row * TH + key // TW
    col = tile_col * TW + key % TW
    bias = jnp.where(live(row, col, margin_ref, plane_rows, plane_cols), 0.0, NEG)
    for i in range(0, TOKENS, 128):
        bias_ref[:TOKENS, i : i + 128] = jnp.where(key == query + i, 0.0, bias)
    padded = bias_ref.shape[0] - TOKENS
    index = lax.broadcasted_iota(jnp.int32, (padded, 128), 0)
    row = jnp.full((padded, 128), -1, jnp.int32)
    col = row
    for start, count, r0, c0, wide, *_ in pieces:
        at = index - start
        down = (at * 171) >> 9 if wide == 3 else at // wide
        here = (at >= 0) & (at < count)
        row = jnp.where(here, tile_row * TH + r0 + down, row)
        col = jnp.where(here, tile_col * TW + c0 + at - down * wide, col)
    is_open = live(row, col, margin_ref, plane_rows, plane_cols)
    is_open = is_open & (row >= 0) & (row < plane_rows) & (col >= 0) & (col < plane_cols)
    bias = jnp.where(is_open, 0.0, NEG)
    for i in range(0, TOKENS, 128):
        bias_ref[TOKENS:, i : i + 128] = bias


def kernel_attend(sizes, n_sample, spans, q_ref, cot_ref, w_ref, bias_ref, place_ref, *refs):
    n_space, grid_cols, plane_rows, plane_cols = sizes
    count = len(spans)
    toks, refs = refs[:count], refs[count + 3 :]
    kv_ref, kvt_ref, nt_ref, pb_ref, grad_ref, keep_ref, send_ref, *refs = refs
    s_s, g_s, ds_s, cm_s, qm_s, dqt_s = refs
    position, member, _, _ = own_ids(grid_cols)
    feat = w_ref.shape[0]
    keys = kv_ref.shape[0]
    padded = keys - TOKENS
    scale = 1.0 / math.sqrt(HEAD)

    parts = [r[...].astype(F32) for r in toks]
    even = (position & 1) == 0
    if paired(sizes):
        parts = [jnp.where(even, parts[1], parts[0]), jnp.where(even, parts[0], parts[1])]
    if spans[-1][1] < padded:
        parts.append(jnp.zeros((padded - spans[-1][1], feat), F32))
    standard, _ = normalise(jnp.concatenate(parts, axis=0))
    normed = standard.astype(BF16)
    for i in range(2):
        part = dot(normed, w_ref[:, (i + 1) * feat : (i + 2) * feat]).astype(BF16)
        kv_ref[TOKENS:, i * feat : (i + 1) * feat] = part
        kvt_ref[i * feat : (i + 1) * feat, TOKENS:] = part.T
    nt_ref[:, TOKENS:] = dot_t(place_ref[...], normed).astype(BF16)
    lane = lax.broadcasted_iota(jnp.int32, (TOKENS, 2 * HEAD), 1)

    def scores(head):
        slot, base = head % 2, head // 2 * 2 * HEAD
        cols = slice(base, base + 2 * HEAD)
        vcols = slice(feat + base, feat + base + 2 * HEAD)
        mine = (lane >= HEAD) if slot else (lane < HEAD)
        out = slice((head % 4) * TOKENS, (head % 4 + 1) * TOKENS)
        q, cot = q_ref[:, cols], cot_ref[:, cols]
        qm_s[out, :] = jnp.where(mine, q, jnp.zeros_like(q))
        cm_s[out, :] = jnp.where(mine, cot, jnp.zeros_like(cot))
        s_s[slot] = dot_t(kv_ref[:, cols], qm_s[out, :])
        g_s[slot] = dot_t(kv_ref[:, vcols], cm_s[out, :])

    def softmax(head):
        slot = head % 2
        out = slice(slot * TOKENS, (slot + 1) * TOKENS)
        top = jnp.full((8, TOKENS), NEG, F32)
        for r in range(0, keys, ROWS):
            x = s_s[slot, r : r + ROWS, :] + bias_ref[r : r + ROWS, :]
            top = jnp.maximum(top, jnp.max(x.reshape(ROWS // 8, 8, TOKENS), axis=0))
        top = jnp.max(top, axis=0, keepdims=True)
        total = jnp.zeros((8, TOKENS), F32)
        delta = jnp.zeros((8, TOKENS), F32)
        for r in range(0, keys, ROWS):
            x = s_s[slot, r : r + ROWS, :] + bias_ref[r : r + ROWS, :]
            e = jnp.exp(x - top)
            s_s[slot, r : r + ROWS, :] = e
            total = total + jnp.sum(e.reshape(ROWS // 8, 8, TOKENS), axis=0)
            eg = e * g_s[slot, r : r + ROWS, :]
            delta = delta + jnp.sum(eg.reshape(ROWS // 8, 8, TOKENS), axis=0)
        inv = 1.0 / jnp.sum(total, axis=0, keepdims=True)
        delta = jnp.sum(delta, axis=0, keepdims=True) * inv
        for r in range(0, keys, ROWS):
            p = s_s[slot, r : r + ROWS, :] * inv
            pb_ref[head // 2, r : r + ROWS, out] = p.astype(BF16)
            ds_s[r : r + ROWS, out] = (p * (g_s[slot, r : r + ROWS, :] - delta)).astype(BF16)

    def products(head):
        row = head * HEAD
        out = slice((head % 2) * TOKENS, (head % 2 + 1) * TOKENS)
        dqt_s[row : row + HEAD, :] = scale * dot(kvt_ref[row : row + HEAD, :], ds_s[:, out])
        if head % 2:
            base = head // 2 * 2 * HEAD
            both = slice((head % 4 - 1) * TOKENS, (head % 4 + 1) * TOKENS)
            grad_ref[:, feat + base : feat + base + 2 * HEAD] = dot(ds_s[...], qm_s[both, :]).astype(BF16)
            grad_ref[:, 2 * feat + base : 2 * feat + base + 2 * HEAD] = dot(
                pb_ref[head // 2], cm_s[both, :]
            ).astype(BF16)

    scores(0)
    for head in range(HEADS):
        if head + 1 < HEADS:
            scores(head + 1)
        softmax(head)
        products(head)
    grad_ref[:TOKENS, :feat] = dqt_s[...].T.astype(BF16)
    grad_ref[TOKENS:, :feat] = jnp.zeros((padded, feat), BF16)

    block = 3 * feat // n_sample
    for j in range(n_sample // 2):
        for target, other in ((keep_ref, 2 * j), (send_ref, 2 * j + 1)):
            cols = pl.ds(pl.multiple_of((member ^ other) * block, 128), block)
            value = dot(nt_ref[...], grad_ref[:, cols])
            target[:, j * block : (j + 1) * block] = value.astype(target.dtype)


def kernel_mix(sizes, spans, kvt_ref, pb_ref, grad_ref, w_ref, att_ref, *refs):
    rim_refs, att_s = refs[:-1], refs[-1]
    feat = att_ref.shape[1]
    even = (lax.axis_index("space") & 1) == 0
    rim = dot_t(grad_ref[TOKENS:, feat:], w_ref[:, feat:])
    if paired(sizes):
        rows = rim_refs[0].shape[0]
        left, right = (rim[lo:hi, :] for lo, hi in spans)
        for ref, value in zip(rim_refs, (jnp.where(even, right, left), jnp.where(even, left, right))):
            wide = feat // 2
            value = jnp.concatenate([value[:, :wide], value[:, wide:]], axis=0).astype(BF16)
            for i in range(3):
                ref[:, i * wide : (i + 1) * wide] = value[i * rows : (i + 1) * rows]
    else:
        for (lo, hi), ref in zip(spans, rim_refs):
            ref[...] = rim[lo:hi, :].astype(BF16)
    for head in range(HEADS):
        row = head * HEAD
        out = slice((head % 2) * TOKENS, (head % 2 + 1) * TOKENS)
        att_s[row : row + HEAD, :] = dot(kvt_ref[feat + row : feat + row + HEAD, :], pb_ref[head // 2, :, out])
    att_ref[...] = att_s[...].T.astype(BF16)


def kernel_own_grad(tok_ref, w_ref, grad_ref, total_ref, standard_ref, inv_ref):
    standard, inv = normalise(tok_ref[...])
    standard_ref[...] = standard
    inv_ref[...] = jnp.broadcast_to(inv, inv_ref.shape)
    total_ref[...] = dot_t(grad_ref[:TOKENS, :], w_ref[...])


def kernel_final(sizes, count, total_ref, standard_ref, inv_ref, index_ref, *refs):
    arrived, out_ref = refs[:count], refs[-1]
    feat = total_ref.shape[1]
    padded = index_ref.shape[1]
    parts = [r[...].astype(F32) for r in arrived]
    if paired(sizes):
        even = (lax.axis_index("space") & 1) == 0
        wide = feat // 2
        parts = [jnp.concatenate([p[:, i * wide : (i + 1) * wide] for i in range(3)], axis=0) for p in parts]
        parts = [jnp.concatenate([p[: p.shape[0] // 2], p[p.shape[0] // 2 :]], axis=1) for p in parts]
        parts = [jnp.where(even, parts[1], parts[0]), jnp.where(even, parts[0], parts[1])]
    have = sum(p.shape[0] for p in parts)
    if have < padded:
        parts.append(jnp.zeros((padded - have, feat), F32))
    rim = jnp.concatenate(parts, axis=0).astype(BF16)
    token = lax.broadcasted_iota(jnp.int32, (TOKENS, padded), 0)
    place = jnp.where(token == index_ref[...], 1.0, 0.0).astype(BF16)
    total = total_ref[...] + dot(place, rim)
    standard = standard_ref[...]
    mean = jnp.mean(total, axis=-1, keepdims=True)
    cross = jnp.mean(total * standard, axis=-1, keepdims=True)
    out_ref[...] = ((total - mean - standard * cross) * inv_ref[:, 0:1]).astype(BF16)


def shift(value, axis, steps):
    count = lax.axis_size(axis)
    first, last = max(0, -steps), min(count, count - steps)
    return lax.ppermute(value, axis, [(i, i + steps) for i in range(first, last)])


def span(step, length):
    if step < 0:
        return (length - HALO, length)
    if step > 0:
        return (0, HALO)
    return (0, length)


def window_span(step, length):
    if step < 0:
        return (-HALO, 0)
    if step > 0:
        return (length, length + HALO)
    return (0, length)


def struct(shape, dtype):
    return jax.ShapeDtypeStruct(shape, dtype)


def pinned(value):
    return pltpu.with_memory_space_constraint(value, pltpu.HBM)


def cost(flops, nbytes, exps=0):
    return pl.CostEstimate(flops=int(flops), bytes_accessed=int(nbytes), transcendentals=int(exps))


def exchange(value, axis, mask):
    count = lax.axis_size(axis)
    return lax.ppermute(value, axis, [(i, i ^ mask) for i in range(count)])


def local(tokens, cotangent, weight, margins):
    feat = weight.shape[0]
    tok, cot = tokens[0, 0], cotangent[0, 0]
    n_space, n_sample = lax.axis_size("space"), lax.axis_size("sample")
    grid_cols = min(8, n_space)
    grid_rows = n_space // grid_cols
    sizes = (n_space, grid_cols, grid_rows * TH, grid_cols * TW)
    masks = row_masks(sizes)
    row_steps = (-1, 0, 1) if grid_rows > 1 else (0,)
    steps = [(r, c) for r in row_steps for c in (-1, 0, 1) if (r, c) != (0, 0)]
    counts, pieces, sources = [], [], []
    way = -1 if paired(sizes) else 1
    for r, c in steps:
        (r0, r1), (c0, c1) = window_span(r, TH), window_span(c, TW)
        pieces.append((sum(counts), (r1 - r0) * (c1 - c0), r0, c0, c1 - c0, span(r, TH)[0], span(c, TW)[0]))
        rr, cc = np.meshgrid(np.arange(*span(way * r, TH)), np.arange(*span(way * c, TW)), indexing="ij")
        sources.append((rr * TW + cc).ravel())
        counts.append(pieces[-1][1])
    halo = sum(counts)
    padded = -(-halo // 128) * 128
    keys = TOKENS + padded
    rim_index = np.concatenate([*sources, np.full(padded - halo, -1)]).astype(np.int32)[None, :]
    ends = np.cumsum([0, *counts])
    spans = [(int(a), int(b)) for a, b in zip(ends[:-1], ends[1:])]

    *rims, tok_near = pl.pallas_call(
        functools.partial(kernel_pack, sizes, pieces),
        out_shape=[*[struct((n, feat), BF16) for n in counts], struct(tok.shape, BF16)],
        in_specs=[hbm()],
        out_specs=[vmem()] * (len(counts) + 1),
        scratch_shapes=[pltpu.SemaphoreType.DMA],
        compiler_params=params(16),
        cost_estimate=cost(2 * halo * TOKENS * feat, 1e6),
        name="pack",
    )(pinned(tok))
    if paired(sizes):
        halo_tokens = [exchange(v, "space", m) for v, m in zip(rims, masks)]
        halo_tokens += [jnp.zeros_like(rims[0])] * (2 - len(masks))
    else:
        halo_tokens = [shift(v, "space", -(r * grid_cols + c)) for v, (r, c) in zip(rims, steps)]

    q, kv, kvt, nt, bias, place, weight = pl.pallas_call(
        functools.partial(kernel_own, sizes, pieces),
        out_shape=(
            struct((TOKENS, feat), BF16),
            struct((keys, 2 * feat), BF16),
            struct((2 * feat, keys), BF16),
            struct((feat, keys), BF16),
            struct((keys, TOKENS), F32),
            struct((feat, feat), BF16),
            struct(weight.shape, BF16),
        ),
        in_specs=[hbm(), vmem(), hbm()],
        out_specs=[vmem()] * 7,
        scratch_shapes=[
            pltpu.SMEM(margins.shape, jnp.int32),
            pltpu.SemaphoreType.DMA((4,)),
        ],
        compiler_params=params(),
        cost_estimate=cost(8 * TOKENS * feat * feat, 7e6),
        name="own",
    )(pinned(margins), tok_near, pinned(weight))

    rim_shape = (2 * counts[0] // 3, 3 * feat // 2)
    outs = pl.pallas_call(
        functools.partial(kernel_attend, sizes, n_sample, spans),
        out_shape=(
            *[struct(a.shape, a.dtype) for a in (kv, kvt, nt)],
            struct((HEADS // 2, keys, 2 * TOKENS), BF16),
            struct((keys, 3 * feat), BF16),
            struct((feat, 3 * feat // 2), F32),
            struct((feat, 3 * feat // 2), BF16),
        ),
        in_specs=[vmem()] * (5 + len(counts) + 3),
        out_specs=[vmem()] * 7,
        input_output_aliases={5 + len(counts) + i: i for i in range(3)},
        scratch_shapes=[
            pltpu.VMEM((2, keys, TOKENS), F32),
            pltpu.VMEM((2, keys, TOKENS), F32),
            pltpu.VMEM((keys, 2 * TOKENS), BF16),
            pltpu.VMEM((4 * TOKENS, 2 * HEAD), BF16),
            pltpu.VMEM((4 * TOKENS, 2 * HEAD), BF16),
            pltpu.VMEM((feat, TOKENS), F32),
        ],
        compiler_params=params(),
        cost_estimate=cost(48 * TOKENS * keys * feat, 6e6, TOKENS * keys * HEADS),
        name="attend",
    )(q, cot, weight, bias, place, *halo_tokens, kv, kvt, nt)
    kvt, prob, grads, keep, send = outs[1], *outs[3:]

    attention, *rims = pl.pallas_call(
        functools.partial(kernel_mix, sizes, spans),
        out_shape=(
            struct((TOKENS, feat), BF16),
            *[struct(rim_shape if paired(sizes) else (n, feat), BF16) for n in counts],
        ),
        in_specs=[vmem()] * 4,
        out_specs=[vmem()] * (1 + len(counts)),
        scratch_shapes=[pltpu.VMEM((feat, TOKENS), F32)],
        compiler_params=params(12),
        cost_estimate=cost(8 * TOKENS * keys * feat, 6e6),
        name="mix",
    )(kvt, prob, grads, weight)

    parts = pl.pallas_call(
        kernel_own_grad,
        out_shape=(struct((TOKENS, feat), F32), struct((TOKENS, feat), F32), struct((TOKENS, 128), F32)),
        in_specs=[vmem()] * 3,
        out_specs=[vmem()] * 3,
        compiler_params=params(12),
        cost_estimate=cost(6 * TOKENS * feat * feat, 5e6),
        name="own_grad",
    )(tok_near, weight, grads)

    total = keep + exchange(send, "sample", 1).astype(F32)
    half = row_split(feat, n_space) * n_space
    first, second = total[:half], total[half:]
    col_masks = [1 << bit for bit in range((n_sample - 1).bit_length() - 1, 0, -1)]
    arrived = []
    if not paired(sizes):
        arrived = [shift(rim, "space", r * grid_cols + c) for (r, c), rim in zip(steps, rims)]

    def cut(value, axis):
        dim = 0 if axis == "space" else 1
        return jnp.split(value, 2, axis=dim)

    upper, lower = first, second
    over_rows = [("space", mask) for mask in masks]
    over_cols = [("sample", mask) for mask in col_masks]
    after, step = [], 0
    for one, two in zip(over_cols + over_rows, over_rows + over_cols):
        upper, out = cut(upper, one[0])
        got = exchange(out.astype(BF16), *one)
        lower, out = cut(lower, two[0])
        out = out.astype(BF16)
        ride = paired(sizes) and two[0] == "space"
        if ride:
            out = jnp.concatenate([out, rims[step]], axis=0)
        other = exchange(out, *two)
        if step in TIES:
            got, other, *parts = lax.optimization_barrier((got, other, *parts))
        if ride:
            arrived.append(other[lower.shape[0] :])
        if step == len(over_cols):
            after.append(got)
        upper = upper + got.astype(F32)
        lower = lower + other[: lower.shape[0]].astype(F32)
        step += 1
    weight_grad = jnp.concatenate([upper, lower], axis=0)

    token_grad = pl.pallas_call(
        functools.partial(kernel_final, sizes, len(steps)),
        out_shape=struct((TOKENS, feat), BF16),
        in_specs=[vmem()] * (4 + len(steps)) + [anywhere()] * len(after),
        out_specs=vmem(),
        compiler_params=params(16),
        cost_estimate=cost(6 * TOKENS * feat * feat, 5e6),
        name="final",
    )(*parts, jnp.asarray(rim_index), *arrived, *after)
    return (attention[None, None], token_grad[None, None], weight_grad)


def solution(mesh):
    return jax.shard_map(
        local,
        mesh=mesh,
        in_specs=(
            P(("groups", "sample"), "space", None, None),
            P(("groups", "sample"), "space", None, None),
            P("groups", None),
            P(("groups", "sample"), None),
        ),
        out_specs=(
            P(("groups", "sample"), "space", None, None),
            P(("groups", "sample"), "space", None, None),
            P(("groups", "space"), "sample"),
        ),
        check_vma=False,
    )
```
